32 devices in a mesh: groups: 2 (over x), seq: 8 (over z, y), chan: 2 (over core).
Axes of the slice: x: 2, y: 2, z: 4, core: 2. Of those that a mesh axis runs over, the one named last changes fastest.
Arguments:
- query_feat: bfloat16 [4096, 2048], P('chan', ('groups', 'seq')), parts along dimension 1, may hold values from -6 to 6
- key_feat: bfloat16 [4096, 2048], P('chan', ('groups', 'seq')), parts along dimension 1, may hold values from -6 to 6
- value_feat: bfloat16 [4096, 2048], P('chan', ('groups', 'seq')), parts along dimension 1, may hold values from -6 to 6
- filter_seed: int32 [16], replicated, may hold values from 1 to 511
- filter_in: float32 [32, 64], replicated, may hold values from -1 to 1
- filter_bias: float32 [64], replicated, may hold values from -3.140625 to 3.140625
- filter_out: float32 [64, 256], P(None, 'chan'), may hold values from -0.75 to 0.75
- decay_rate: float32 [256], P('chan'), may hold values from 0.000390625 to 0.0078125
- reach_blocks: int32 [256], P('chan'), may hold values from 1 to 2, as said below
- skip_gain: float32 [4096], P('chan'), may hold values from -4 to 4
- out_weight: bfloat16 [4096, 2048], P('chan'), may hold values from -0.09375 to 0.09375
Outputs:
- projected: bfloat16 [2048, 2048], P(('groups', 'seq'), 'chan'), parts along dimension 0
The draws below stay inside these ranges and needn't reach their ends.
There are 2 independent parts, one for each index of `groups`. The reference program is written for one: setup_inputs(seed, part) draws one part's arguments, and reference() takes and returns one part's arrays. A program takes and returns all parts, laid end to end along the dimension named above; an argument that names none is the same for every part. Nothing has to cross between parts.
Inputs may be any that keep to these rules, and one draw needn't show every extreme that they name: `reach_blocks`: some filter group reaches 2 blocks and some filter group only one.
All inputs are finite; a program needn't handle non-finite values.
Results may differ from the reference program's by a relative error of at most 0.0059.
Values may be sent and summed in bfloat16 or wider, within the bound.
A program may use at most 128 MiB of HBM per device.

```python
import math
import jax
import jax.numpy as jnp
from jax import lax

MODEL_DIM = 4096
FILTER_GROUPS = 256
OUT_COLS = 2048
POS_FREQS = 16
FILTER_HID = 64
BLOCK_TOK = 128
REACH_MAX = 2
SEQ_LEN = 1024


def draw_reach_blocks(key, part):
    values = jax.random.randint(jax.random.fold_in(key, 11), (FILTER_GROUPS,), 1, REACH_MAX + 1)
    top_place = jax.random.randint(jax.random.fold_in(key, 12), (), 0, FILTER_GROUPS)
    low_place = (top_place + jax.random.randint(jax.random.fold_in(key, 13), (), 1, FILTER_GROUPS)) % FILTER_GROUPS
    index = lax.iota(jnp.int32, FILTER_GROUPS)
    values = jnp.where(index == top_place, REACH_MAX, values)
    values = jnp.where(index == low_place, 1, values)
    return values.astype(jnp.int32)


def with_ends(entries, rng, smallest, largest):
    index_at = [jax.random.randint(jax.random.fold_in(rng, axis), (), 0, length) for axis, length in enumerate(entries.shape)]
    main_axis = entries.shape.index(max(entries.shape))
    neighbour = index_at[:main_axis] + [(index_at[main_axis] + 1) % entries.shape[main_axis]] + index_at[main_axis + 1:]
    return entries.at[tuple(index_at)].set(smallest).at[tuple(neighbour)].set(largest)


def shard_levels(own_key, dims, split, low, high):
    def one(position, parts):
        draws = jax.random.uniform(jax.random.fold_in(jax.random.fold_in(own_key, 6), position), (parts,), jnp.float32, low / len(split), high / len(split))
        return jnp.repeat(jnp.exp(draws), dims[position] // parts).reshape((-1,) + (1,) * (len(dims) - position - 1))

    gain = one(*split[0])
    for cut in split[1:]:
        gain = gain * one(*cut)
    return gain


def scatter_about(own_key, dims, width, most, cuts=(), dtype=jnp.bfloat16):
    array = jax.random.normal(own_key, dims, jnp.float32) * width
    if len(cuts) > 0:
        array = shard_levels(own_key, dims, cuts, -0.22, 0.18) * array
    return jnp.clip(array, min=-most, max=most).astype(dtype)


def setup_inputs(seed: int = 0, part: int = 0) -> dict:
    arg_keys = jax.random.split(jax.random.key(seed), 12)
    part_keys = jax.random.split(jax.random.fold_in(arg_keys[11], part), 12)
    return {
        "query_feat": scatter_about(part_keys[0], (MODEL_DIM, SEQ_LEN), 1.0, 6.0, ((0, 2), (1, 8))),
        "key_feat": scatter_about(part_keys[1], (MODEL_DIM, SEQ_LEN), 1.0, 6.0, ((0, 2), (1, 8))),
        "value_feat": scatter_about(part_keys[2], (MODEL_DIM, SEQ_LEN), 1.0, 6.0, ((0, 2), (1, 8))),
        "filter_seed": with_ends(jax.random.randint(arg_keys[3], (POS_FREQS,), 1, SEQ_LEN // 2), jax.random.fold_in(arg_keys[3], 1), 1, (SEQ_LEN // 2) - 1).astype(jnp.int32),
        "filter_in": scatter_about(arg_keys[4], (2 * POS_FREQS, FILTER_HID), (2 * POS_FREQS) ** -0.5, 1.0, (), jnp.float32),
        "filter_bias": jnp.clip(jax.random.uniform(arg_keys[5], (FILTER_HID,), jnp.float32, -3.140625, 3.140625), -3.140625, 3.140625),
        "filter_out": scatter_about(arg_keys[6], (FILTER_HID, FILTER_GROUPS), FILTER_HID ** -0.5, 0.75, ((1, 2),), jnp.float32),
        "decay_rate": jnp.clip(jnp.exp(math.log(0.0078125) - 2.9957323 * jax.random.uniform(arg_keys[7], (FILTER_GROUPS,), jnp.float32) ** shard_levels(arg_keys[7], (FILTER_GROUPS,), ((0, 2),), -0.2, 0.2)), 0.000390625, 0.0078125),
        "reach_blocks": draw_reach_blocks(jax.random.fold_in(arg_keys[11], 71), part),
        "skip_gain": scatter_about(arg_keys[9], (MODEL_DIM,), 1.0, 4.0, ((0, 2),), jnp.float32),
        "out_weight": scatter_about(arg_keys[10], (MODEL_DIM, OUT_COLS), MODEL_DIM ** -0.5, 0.09375, ((0, 2),)),
    }


def reference(query_feat, key_feat, value_feat, filter_seed, filter_in, filter_bias, filter_out, decay_rate, reach_blocks, skip_gain, out_weight):
    product = (key_feat.astype(jnp.float32) * value_feat.astype(jnp.float32)).astype(jnp.bfloat16)
    lag_index = lax.iota(jnp.int32, REACH_MAX * BLOCK_TOK)
    phases = lag_index[:, None] * filter_seed[None, :] % SEQ_LEN
    angles = phases.astype(jnp.float32) * (2.0 * math.pi / SEQ_LEN)
    features = jnp.concatenate([jnp.cos(angles), jnp.sin(angles)], axis=1)
    hidden = jnp.sin(jnp.dot(features, filter_in, precision=lax.Precision.HIGHEST, preferred_element_type=jnp.float32) + filter_bias)
    shaped = jnp.dot(hidden, filter_out, precision=lax.Precision.HIGHEST, preferred_element_type=jnp.float32)
    envelope = jnp.exp(-decay_rate[None, :] * lag_index.astype(jnp.float32)[:, None]) * (1.0 / math.sqrt(REACH_MAX * BLOCK_TOK))
    inside = lag_index[:, None] < reach_blocks[None, :] * BLOCK_TOK
    taps = jnp.where(inside, shaped * envelope, 0.0).astype(jnp.bfloat16)
    per_group = MODEL_DIM // FILTER_GROUPS
    fft_len = 2 * SEQ_LEN

    def convolve(inputs_pair):
        channel_rows, tap_row = inputs_pair
        spectrum = jnp.fft.rfft(channel_rows.astype(jnp.float32), n=fft_len, axis=1) * jnp.fft.rfft(tap_row.astype(jnp.float32), n=fft_len)[None, :]
        return jnp.fft.irfft(spectrum, n=fft_len, axis=1)[:, :SEQ_LEN]
    convolved = lax.map(convolve, (product.reshape(FILTER_GROUPS, per_group, SEQ_LEN), taps.T)).reshape(MODEL_DIM, SEQ_LEN)
    mixed = convolved + skip_gain[:, None] * product.astype(jnp.float32)
    gated = (query_feat.astype(jnp.float32) * mixed).astype(jnp.bfloat16)
    projected = lax.dot_general(gated, out_weight, (((0,), (0,)), ((), ())), preferred_element_type=jnp.float32)
    return projected.astype(jnp.bfloat16)
```

```python
import functools
import math

import jax
import jax.numpy as jnp
from jax import lax
from jax.experimental import pallas as pl
from jax.experimental.pallas import tpu as pltpu
from jax.sharding import PartitionSpec as P

MESH = pl.DeviceIdType.MESH
CHUNK = 256
PIECE = 128
LAST = 64
DIRECT = 0
PARTS = 2


def as_column(row, size):
    rows = lax.broadcasted_iota(jnp.int32, (size, size), 0)
    cols = lax.broadcasted_iota(jnp.int32, (size, size), 1)
    spread = jnp.broadcast_to(row, (size, size))
    return jnp.sum(jnp.where(rows == cols, spread, 0.0), axis=1, keepdims=True)


def halo_kernel(
    seq_count,
    query_hbm,
    key_hbm,
    value_hbm,
    seed_hbm,
    in_hbm,
    bias_hbm,
    fout_hbm,
    decay_hbm,
    reach_hbm,
    skip_hbm,
    weight_hbm,
    out_ref,
    seed_ref,
    in_ref,
    bias_ref,
    fout_ref,
    decay_ref,
    reach_ref,
    skip_ref,
    query,
    factors,
    weight,
    product,
    back,
    taps,
    toeplitz,
    skip_wide,
    gated,
    total,
    part_out,
    part_in,
    small_sem,
    factor_sem,
    query_sem,
    weight_sem,
    send_sem,
    arrive_sem,
    core_send,
    core_recv,
):
    channels, block = product.shape
    filters = taps.shape[0]
    per_group = channels // filters
    lags = taps.shape[1]
    chunks = channels // CHUNK
    halves = CHUNK // PIECE
    groups_piece = PIECE // per_group
    cols = out_ref.shape[1]
    seq_len = seq_count * block
    whole = (channels - CHUNK) // PIECE
    tail = piece_tail(channels)
    pieces = whole + len(tail)
    relayed = sum(n * PIECE < channels - DIRECT for n in range(whole)) + sum(
        offset < channels - DIRECT for offset, _ in tail
    )

    me = lax.axis_index("seq")
    core = lax.axis_index("chan")
    pair = me // 2
    odd = me % 2
    mate = me + 1 - 2 * odd
    other = 1 - core
    has_low = pair > 0
    has_high = pair < seq_count // 2 - 1
    even = odd == 0
    relays = jnp.logical_and(has_low, odd == 1)
    from_direct = jnp.logical_and(has_low, even)
    to_direct = jnp.logical_and(has_high, odd == 1)

    barrier = pltpu.get_barrier_semaphore()

    def greet(device):
        pl.semaphore_signal(barrier, inc=1, device_id=device, device_id_type=MESH)

    greet({"chan": other})
    pl.when(jnp.logical_or(odd == 1, has_low))(lambda: greet({"seq": mate}))
    pl.when(has_low)(lambda: greet({"seq": me - 2}))
    receivers = 1 + jnp.logical_or(even, has_low).astype(jnp.int32) + has_high.astype(jnp.int32)
    if relayed < pieces:
        pl.when(from_direct)(lambda: greet({"seq": me - 1}))
        receivers = receivers + to_direct.astype(jnp.int32)

    def rows_of(k):
        return pl.ds(pl.multiple_of(k * CHUNK, CHUNK), CHUNK)

    def piece_of(n):
        if isinstance(n, int) and n >= whole:
            return pl.ds(*tail[n - whole])
        return pl.ds(pl.multiple_of(n * PIECE, PIECE), PIECE)

    def load_weight(k):
        return pltpu.make_async_copy(
            weight_hbm.at[rows_of(k)], weight.at[rows_of(k)], weight_sem.at[k % 2]
        )

    load_key = pltpu.make_async_copy(key_hbm, factors.at[0], factor_sem)
    load_value = pltpu.make_async_copy(value_hbm, factors.at[1], factor_sem)
    load_query = pltpu.make_async_copy(query_hbm, query, query_sem)

    def far_copy(rows, n):
        return pltpu.make_async_remote_copy(
            src_ref=product.at[rows],
            dst_ref=back.at[0, rows],
            send_sem=send_sem.at[0],
            recv_sem=arrive_sem.at[n],
            device_id={"seq": me + 2},
            device_id_type=MESH,
        )

    def near_copy(rows, n):
        return pltpu.make_async_remote_copy(
            src_ref=product.at[rows],
            dst_ref=back.at[1, rows],
            send_sem=send_sem.at[1],
            recv_sem=arrive_sem.at[n],
            device_id={"seq": mate},
            device_id_type=MESH,
        )

    def relay_copy(rows, n):
        return pltpu.make_async_remote_copy(
            src_ref=back.at[0, rows],
            dst_ref=back.at[1, rows],
            send_sem=send_sem.at[1],
            recv_sem=arrive_sem.at[n],
            device_id={"seq": mate},
            device_id_type=MESH,
        )

    def direct_copy(rows, n):
        return pltpu.make_async_remote_copy(
            src_ref=product.at[rows],
            dst_ref=back.at[1, rows],
            send_sem=send_sem.at[2],
            recv_sem=arrive_sem.at[n],
            device_id={"seq": me + 1},
            device_id_type=MESH,
        )

    load_key.start()
    load_value.start()
    small = [
        pltpu.make_async_copy(source, target, small_sem.at[i])
        for i, (source, target) in enumerate(
            (
                (seed_hbm, seed_ref),
                (in_hbm, in_ref),
                (bias_hbm, bias_ref),
                (fout_hbm, fout_ref),
                (decay_hbm, decay_ref),
                (reach_hbm, reach_ref),
                (skip_hbm, skip_ref),
            )
        )
    ]
    for copy in small:
        copy.start()

    def start_sends(first, last):
        @pl.when(has_high)
        def _():
            for n in range(first, min(last, relayed)):
                far_copy(piece_of(n), n).start()

        @pl.when(even)
        def _():
            for n in range(first, last):
                near_copy(piece_of(n), n).start()

    pltpu.make_async_copy(factors, factors, factor_sem).wait()
    for k in range(chunks):
        rows = slice(k * CHUNK, (k + 1) * CHUNK)
        part = factors[0, rows].astype(jnp.float32) * factors[1, rows].astype(jnp.float32)
        product[rows] = part.astype(jnp.bfloat16)
        if k == 0:
            pl.semaphore_wait(barrier, receivers)
        start_sends(k * halves, (k + 1) * halves if k < chunks - 1 else pieces)

    if relayed < pieces:

        @pl.when(to_direct)
        def _():
            for n in range(relayed, pieces):
                direct_copy(piece_of(n), n).start()

        @pl.when(has_high)
        def _():
            for n in range(relayed, pieces):
                far_copy(piece_of(n), n).start()

    load_query.start()
    load_weight(0).start()
    for copy in small:
        copy.wait()

    @pl.when(jnp.logical_not(has_low))
    def _():
        back[0] = jnp.zeros_like(back[0])

    @pl.when(me == 0)
    def _():
        back[1] = jnp.zeros_like(back[1])

    freqs = in_ref.shape[0] // 2
    hidden_count = in_ref.shape[1]
    lag = lax.broadcasted_iota(jnp.int32, (freqs, lags), 1)
    seeds = as_column(seed_ref[...].astype(jnp.float32), freqs).astype(jnp.int32)
    angles = ((seeds * lag) & (seq_len - 1)).astype(jnp.float32) * (2.0 * math.pi / seq_len)
    features = jnp.concatenate([jnp.cos(angles), jnp.sin(angles)], axis=0)
    first_dims = (((0,), (0,)), ((), ()))
    hidden = jnp.sin(
        lax.dot_general(
            in_ref[...],
            features,
            first_dims,
            precision=lax.Precision.HIGHEST,
            preferred_element_type=jnp.float32,
        )
        + as_column(bias_ref[...], hidden_count)
    )
    shaped = lax.dot_general(
        fout_ref[...],
        hidden,
        first_dims,
        precision=lax.Precision.HIGHEST,
        preferred_element_type=jnp.float32,
    )
    lag = lax.broadcasted_iota(jnp.int32, (filters, lags), 1).astype(jnp.float32)
    envelope = jnp.exp(-as_column(decay_ref[...], filters) * lag) * (1.0 / math.sqrt(lags))
    inside = lag < as_column(reach_ref[...].astype(jnp.float32), filters) * block
    taps[...] = (
        jnp.where(inside, shaped * envelope, 0.0).astype(jnp.bfloat16).astype(jnp.float32)
    )

    total[...] = jnp.zeros_like(total)
    load_query.wait()
    source_tok = lax.broadcasted_iota(jnp.int32, (block, block), 0)
    target_tok = lax.broadcasted_iota(jnp.int32, (block, block), 1)
    upper = target_tok >= source_tok

    def spread(row):
        return pltpu.roll(
            jnp.broadcast_to(row, (block, block)), 0, 1, stride=1, stride_axis=0
        ).astype(jnp.bfloat16)

    def band(group):
        tap_row = taps[pl.ds(group, 1), :]
        low = spread(tap_row[:, :block])
        high = spread(tap_row[:, block:])
        zero = jnp.zeros_like(low)
        return (
            jnp.where(upper, zero, high),
            jnp.where(upper, high, low),
            jnp.where(upper, low, zero),
        )

    def skip_rows(n):
        return jnp.broadcast_to(skip_ref[pl.ds(n, 1), :], (PIECE, PIECE)).T

    for n in range(halves):
        skip_wide[n * PIECE : (n + 1) * PIECE, :] = skip_rows(whole + n)
    for j in range(CHUNK // per_group):
        for i, part in enumerate(band(whole * groups_piece + j)):
            toeplitz[j, i * block : (i + 1) * block] = part

    def arrive(n):
        rows = piece_of(n)

        @pl.when(has_low)
        def _():
            both = back.at[:, rows]
            pltpu.make_async_copy(both, both, arrive_sem.at[n]).wait()

        @pl.when(me == 1)
        def _():
            near_copy(rows, n).wait_recv()

        if isinstance(n, int):
            if n < relayed:
                pl.when(relays)(lambda: relay_copy(rows, n).start())
        else:

            @pl.when(jnp.logical_and(relays, n < relayed))
            def _():
                relay_copy(rows, n).start()

    def gate(row, matrix, skip, place):
        rows = pl.ds(pl.multiple_of(row, per_group), per_group)
        own = product[rows, :]
        window = jnp.concatenate([back[0, rows, :], back[1, rows, :], own], axis=1)
        mixed = jnp.dot(window, matrix, preferred_element_type=jnp.float32)
        mixed = mixed + skip * own.astype(jnp.float32)
        gated[place : place + per_group, :] = (query[rows, :].astype(jnp.float32) * mixed).astype(
            jnp.bfloat16
        )

    @pl.loop(0, chunks - 1)
    def _(k):
        load_weight(k + 1).start()
        for half in range(halves):
            n = k * halves + half
            arrive(n)
            skip = skip_rows(n)
            for j in range(groups_piece):
                start = j * per_group
                matrix = jnp.concatenate(band(n * groups_piece + j), axis=0)
                gate(
                    n * PIECE + start,
                    matrix,
                    skip[start : start + per_group],
                    half * PIECE + start,
                )
        load_weight(k).wait()
        chunk = gated[...].T
        for half in range(2):
            total[half] += jnp.dot(
                chunk,
                weight[rows_of(k), half * cols : (half + 1) * cols],
                preferred_element_type=jnp.float32,
            )

    load_weight(chunks - 1).wait()
    for i, (offset, size) in enumerate(tail):
        arrive(whole + i)
        for row in range(offset, offset + size, per_group):
            place = row - (channels - CHUNK)
            gate(row, toeplitz[place // per_group], skip_wide[place : place + per_group, :], place)

    chunk = gated[...].T
    last_rows = slice(channels - CHUNK, channels)

    def last(half, part):
        width = cols // PARTS
        columns = pl.ds(pl.multiple_of(half * cols + part * width, width), width)
        here = slice(part * width, (part + 1) * width)
        return total[half, :, here] + jnp.dot(
            chunk, weight[last_rows, columns], preferred_element_type=jnp.float32
        )

    def core_copy(part):
        return pltpu.make_async_remote_copy(
            src_ref=part_out.at[part],
            dst_ref=part_in.at[part],
            send_sem=core_send,
            recv_sem=core_recv.at[part],
            device_id={"chan": other},
            device_id_type=MESH,
        )

    for part in range(PARTS):
        part_out[part] = last(other, part).astype(jnp.bfloat16)
        core_copy(part).start()
    for part in range(PARTS):
        total[core, :, part * (cols // PARTS) : (part + 1) * (cols // PARTS)] = last(core, part)

    everything = slice(0, channels)

    @pl.when(has_high)
    def _():
        far_copy(everything, 0).wait_send()

    @pl.when(even)
    def _():
        near_copy(everything, 0).wait_send()

    @pl.when(relays)
    def _():
        relay_copy(slice(0, channels - DIRECT), 0).wait_send()

    if relayed < pieces:

        @pl.when(to_direct)
        def _():
            direct_copy(slice(channels - DIRECT, channels), 0).wait_send()

    pltpu.make_async_copy(part_out, part_out, core_send).wait()
    for part in range(PARTS):
        here = slice(part * (cols // PARTS), (part + 1) * (cols // PARTS))
        core_copy(part).wait_recv()
        out_ref[:, here] = (total[core, :, here] + part_in[part].astype(jnp.float32)).astype(
            jnp.bfloat16
        )


def piece_tail(channels):
    start = channels - CHUNK
    sizes = [PIECE] + [LAST] * ((CHUNK - PIECE) // LAST)
    return [(start + sum(sizes[:i]), size) for i, size in enumerate(sizes)]


def halo_body(
    query_feat,
    key_feat,
    value_feat,
    filter_seed,
    filter_in,
    filter_bias,
    filter_out,
    decay_rate,
    reach_blocks,
    skip_gain,
    out_weight,
):
    channels, block = query_feat.shape
    seq_count = lax.axis_size("seq")
    filters = decay_rate.shape[0]
    cols = out_weight.shape[1] // 2
    pieces = (channels - CHUNK) // PIECE + len(piece_tail(channels))
    small = (
        filter_seed.reshape(1, -1),
        filter_in,
        filter_bias.reshape(1, -1),
        filter_out,
        decay_rate.reshape(1, -1),
        reach_blocks.reshape(1, -1),
        skip_gain.reshape(-1, 128),
    )
    lags = block * 2
    return pl.pallas_call(
        functools.partial(halo_kernel, seq_count),
        out_shape=pltpu.VMEM((block, cols), jnp.bfloat16),
        in_specs=[pl.BlockSpec(memory_space=pltpu.HBM)] * 11,
        out_specs=pl.BlockSpec(memory_space=pltpu.VMEM),
        scratch_shapes=[
            *[pltpu.VMEM(array.shape, array.dtype) for array in small],
            pltpu.VMEM((channels, block), jnp.bfloat16),
            pltpu.VMEM((2, channels, block), jnp.bfloat16),
            pltpu.VMEM(out_weight.shape, jnp.bfloat16),
            pltpu.VMEM((channels, block), jnp.bfloat16),
            pltpu.VMEM((2, channels, block), jnp.bfloat16),
            pltpu.VMEM((filters, lags), jnp.float32),
            pltpu.VMEM((CHUNK * filters // channels, 3 * block, block), jnp.bfloat16),
            pltpu.VMEM((CHUNK, block), jnp.float32),
            pltpu.VMEM((CHUNK, block), jnp.bfloat16),
            pltpu.VMEM((2, block, cols), jnp.float32),
            pltpu.VMEM((PARTS, block, cols // PARTS), jnp.bfloat16),
            pltpu.VMEM((PARTS, block, cols // PARTS), jnp.bfloat16),
            pltpu.SemaphoreType.DMA((len(small),)),
            pltpu.SemaphoreType.DMA,
            pltpu.SemaphoreType.DMA,
            pltpu.SemaphoreType.DMA((2,)),
            pltpu.SemaphoreType.DMA((3,)),
            pltpu.SemaphoreType.DMA((pieces,)),
            pltpu.SemaphoreType.DMA,
            pltpu.SemaphoreType.DMA((PARTS,)),
        ],
        compiler_params=pltpu.CompilerParams(
            collective_id=0, has_side_effects=True, vmem_limit_bytes=32 * 2**20
        ),
        name="halo_conv_project",
    )(
        *(
            pltpu.with_memory_space_constraint(array, pltpu.HBM)
            for array in (query_feat, key_feat, value_feat, *small, out_weight)
        )
    )


def filter_rows(
    lag_index,
    filter_seed,
    filter_in,
    filter_bias,
    filter_out,
    decay_rate,
    reach_blocks,
    block_len,
    seq_len,
    reach_max,
):
    safe_lag = jnp.maximum(lag_index, 0)
    phases = safe_lag[:, None] * filter_seed[None, :] % seq_len
    angles = phases.astype(jnp.float32) * (2.0 * math.pi / seq_len)
    features = jnp.concatenate([jnp.cos(angles), jnp.sin(angles)], axis=1)
    hidden = jnp.sin(
        jnp.dot(
            features, filter_in, precision=lax.Precision.HIGHEST, preferred_element_type=jnp.float32
        )
        + filter_bias
    )
    shaped = jnp.dot(
        hidden, filter_out, precision=lax.Precision.HIGHEST, preferred_element_type=jnp.float32
    )
    envelope = jnp.exp(-decay_rate[None, :] * safe_lag.astype(jnp.float32)[:, None]) * (
        1.0 / math.sqrt(reach_max * block_len)
    )
    inside = (lag_index[:, None] >= 0) & (lag_index[:, None] < reach_blocks[None, :] * block_len)
    return jnp.where(inside, shaped * envelope, 0.0).astype(jnp.bfloat16)


def hankel_rows(tap_rows, sub_len, span_len):
    return jnp.stack(
        [
            tap_rows[:, sub_len - 1 - offset : sub_len - 1 - offset + span_len]
            for offset in range(sub_len)
        ],
        axis=1,
    )


def body(
    query_feat,
    key_feat,
    value_feat,
    filter_seed,
    filter_in,
    filter_bias,
    filter_out,
    decay_rate,
    reach_blocks,
    skip_gain,
    out_weight,
):
    channels, block = query_feat.shape
    seq_count = lax.axis_size("seq")
    reach_max = seq_count // 4
    seq_len = block * seq_count
    sub_len = min(128, block)
    span_len = reach_max * block + sub_len
    rev_len = span_len + sub_len - 1
    filter_count = decay_rate.shape[0]
    per_group = channels // filter_count
    product = (key_feat.astype(jnp.float32) * value_feat.astype(jnp.float32)).astype(jnp.bfloat16)
    lag_index = reach_max * block + sub_len - 1 - lax.iota(jnp.int32, rev_len)
    taps = filter_rows(
        lag_index,
        filter_seed,
        filter_in,
        filter_bias,
        filter_out,
        decay_rate,
        reach_blocks,
        block,
        seq_len,
        reach_max,
    ).T
    seq_index = lax.axis_index("seq")
    spread, query_all = (
        lax.all_to_all(product, "seq", split_axis=0, concat_axis=1, tiled=True),
        lax.all_to_all(query_feat, "seq", split_axis=0, concat_axis=1, tiled=True),
    )
    chan_dev = spread.shape[0]
    full_len = spread.shape[1]
    padded = jnp.concatenate(
        [jnp.zeros((chan_dev, reach_max * block), jnp.bfloat16), spread], axis=1
    )
    pieces = padded.reshape(chan_dev, -1, sub_len)
    count_tiles = full_len // sub_len
    span_blocks = span_len // sub_len
    windows = jnp.concatenate([pieces[:, k : k + count_tiles] for k in range(span_blocks)], axis=2)
    first_chan = seq_index * chan_dev
    group_ids = (first_chan + lax.iota(jnp.int32, chan_dev)) // per_group
    chan_taps = jnp.take(taps, group_ids, axis=0)
    chan_block = math.gcd(8, chan_dev)
    windows = windows.reshape(chan_dev // chan_block, chan_block, count_tiles, span_len)
    chan_taps = chan_taps.reshape(chan_dev // chan_block, chan_block, rev_len)

    def convolve_chan(inputs_pair):
        window_part, tap_part = inputs_pair
        hankel = hankel_rows(tap_part, sub_len, span_len)
        return jnp.einsum("ctw,caw->cta", window_part, hankel, preferred_element_type=jnp.float32)

    convolved = lax.map(convolve_chan, (windows, chan_taps))
    convolved = convolved.reshape(chan_dev, full_len)
    skip_part = lax.dynamic_slice_in_dim(skip_gain, first_chan, chan_dev)
    mixed_part = convolved + skip_part[:, None] * spread.astype(jnp.float32)
    gated_part = (query_all.astype(jnp.float32) * mixed_part).astype(jnp.bfloat16)
    gated = lax.all_to_all(gated_part, "seq", split_axis=1, concat_axis=0, tiled=True)
    reduced = lax.psum_scatter(
        lax.dot_general(
            out_weight, gated, (((0,), (0,)), ((), ())), preferred_element_type=jnp.float32
        ),
        "chan",
        scatter_dimension=0,
        tiled=True,
    )
    return reduced.T.astype(jnp.bfloat16)


def solution(mesh):
    halo = mesh.shape["seq"] // 4 == 2 and mesh.shape["chan"] == 2
    return jax.shard_map(
        halo_body if halo else body,
        mesh=mesh,
        in_specs=(
            P("chan", ("groups", "seq")),
            P("chan", ("groups", "seq")),
            P("chan", ("groups", "seq")),
            P(),
            P(),
            P(),
            P(None, "chan"),
            P("chan"),
            P("chan"),
            P("chan"),
            P("chan", None),
        ),
        out_specs=P(("groups", "seq"), "chan"),
        check_vma=False,
    )
```

```python
import functools
import math

import jax
import jax.numpy as jnp
from jax import lax
from jax.experimental import pallas as pl
from jax.experimental.pallas import tpu as pltpu
from jax.sharding import PartitionSpec as P

MESH = pl.DeviceIdType.MESH
CHUNK = 256
PIECE = 128
LAST = 64
EARLY = 8


def as_column(row, size):
    rows = lax.broadcasted_iota(jnp.int32, (size, size), 0)
    cols = lax.broadcasted_iota(jnp.int32, (size, size), 1)
    spread = jnp.broadcast_to(row, (size, size))
    return jnp.sum(jnp.where(rows == cols, spread, 0.0), axis=1, keepdims=True)


def halo_kernel(
    seq_count,
    query_hbm,
    key_hbm,
    value_hbm,
    seed_hbm,
    in_hbm,
    bias_hbm,
    fout_hbm,
    decay_hbm,
    reach_hbm,
    skip_hbm,
    weight_hbm,
    out_ref,
    seed_ref,
    in_ref,
    bias_ref,
    fout_ref,
    decay_ref,
    reach_ref,
    skip_ref,
    query,
    factors,
    weight,
    product,
    back,
    lifted,
    taps,
    toeplitz,
    skip_wide,
    gated,
    gated_tail,
    weight_in,
    total,
    part_out,
    part_in,
    small_sem,
    factor_sem,
    query_sem,
    weight_sem,
    send_sem,
    arrive_sem,
    lift_sem,
    core_send,
    core_recv,
):
    channels, block = product.shape
    filters = taps.shape[0]
    per_group = channels // filters
    lags = taps.shape[1]
    chunks = channels // CHUNK
    halves = CHUNK // PIECE
    groups_piece = PIECE // per_group
    cols = out_ref.shape[1]
    seq_len = seq_count * block
    whole = (channels - CHUNK) // PIECE
    tail = piece_tail(channels)
    pieces = whole + len(tail)
    carried = list(range(whole - halves, whole))
    carried_rows = slice(channels - 2 * CHUNK, channels - CHUNK)
    order = [n for n in range(pieces) if n not in carried] + carried

    me = lax.axis_index("seq")
    core = lax.axis_index("chan")
    pair = me // 2
    odd = me % 2
    mate = me + 1 - 2 * odd
    other = 1 - core
    has_low = pair > 0
    has_high = pair < seq_count // 2 - 1
    even = odd == 0
    relays = jnp.logical_and(has_low, odd == 1)
    carries = jnp.logical_and(has_high, even)

    barrier = pltpu.get_barrier_semaphore()

    def greet(device):
        pl.semaphore_signal(barrier, inc=1, device_id=device, device_id_type=MESH)

    greet({"chan": other})
    greet({"seq": mate})
    pl.when(has_low)(lambda: greet({"seq": me - 2}))
    receivers = 2 + has_high.astype(jnp.int32)

    def rows_of(k):
        return pl.ds(pl.multiple_of(k * CHUNK, CHUNK), CHUNK)

    def piece_of(n):
        if isinstance(n, int) and n >= whole:
            return pl.ds(*tail[n - whole])
        return pl.ds(pl.multiple_of(n * PIECE, PIECE), PIECE)

    def load_weight(k):
        return pltpu.make_async_copy(
            weight_hbm.at[rows_of(k)], weight.at[rows_of(k)], weight_sem.at[k % 2]
        )

    load_key = pltpu.make_async_copy(key_hbm, factors.at[0], factor_sem)
    load_value = pltpu.make_async_copy(value_hbm, factors.at[1], factor_sem)
    load_query = pltpu.make_async_copy(query_hbm, query, query_sem)

    def far_copy(rows, n):
        return pltpu.make_async_remote_copy(
            src_ref=product.at[rows],
            dst_ref=back.at[0, rows],
            send_sem=send_sem.at[0],
            recv_sem=arrive_sem.at[n],
            device_id={"seq": me + 2},
            device_id_type=MESH,
        )

    def near_copy(rows, n):
        return pltpu.make_async_remote_copy(
            src_ref=product.at[rows],
            dst_ref=back.at[1, rows],
            send_sem=send_sem.at[1],
            recv_sem=arrive_sem.at[n],
            device_id={"seq": mate},
            device_id_type=MESH,
        )

    def relay_copy(rows, n):
        return pltpu.make_async_remote_copy(
            src_ref=back.at[0, rows],
            dst_ref=back.at[1, rows],
            send_sem=send_sem.at[1],
            recv_sem=arrive_sem.at[n],
            device_id={"seq": mate},
            device_id_type=MESH,
        )

    def lift_copy():
        return pltpu.make_async_remote_copy(
            src_ref=product.at[carried_rows],
            dst_ref=lifted,
            send_sem=send_sem.at[2],
            recv_sem=lift_sem,
            device_id={"seq": mate},
            device_id_type=MESH,
        )

    def carry_copy(i):
        return pltpu.make_async_remote_copy(
            src_ref=lifted.at[pl.ds(i * PIECE, PIECE)],
            dst_ref=back.at[1, piece_of(carried[i])],
            send_sem=send_sem.at[2],
            recv_sem=arrive_sem.at[carried[i]],
            device_id={"seq": me + 2},
            device_id_type=MESH,
        )

    last_rows = slice(channels - CHUNK, channels)

    def half_cols(half):
        return pl.ds(pl.multiple_of(half * cols, cols), cols)

    weight_copy = pltpu.make_async_remote_copy(
        src_ref=weight_hbm.at[last_rows, half_cols(other)],
        dst_ref=weight_in,
        send_sem=core_send.at[0],
        recv_sem=core_recv.at[0],
        device_id={"chan": other},
        device_id_type=MESH,
    )
    part_copy = pltpu.make_async_remote_copy(
        src_ref=part_out,
        dst_ref=part_in,
        send_sem=core_send.at[1],
        recv_sem=core_recv.at[1],
        device_id={"chan": other},
        device_id_type=MESH,
    )

    def gated_copy(rows, i):
        return pltpu.make_async_remote_copy(
            src_ref=gated_tail.at[0, rows],
            dst_ref=gated_tail.at[1, rows],
            send_sem=core_send.at[2],
            recv_sem=core_recv.at[2 + i],
            device_id={"chan": other},
            device_id_type=MESH,
        )

    load_key.start()
    load_value.start()
    small = [
        pltpu.make_async_copy(source, target, small_sem.at[i])
        for i, (source, target) in enumerate(
            (
                (seed_hbm, seed_ref),
                (in_hbm, in_ref),
                (bias_hbm, bias_ref),
                (fout_hbm, fout_ref),
                (decay_hbm, decay_ref),
                (reach_hbm, reach_ref),
                (skip_hbm, skip_ref),
            )
        )
    ]
    for copy in small:
        copy.start()

    pltpu.make_async_copy(factors, factors, factor_sem).wait()

    def multiply(rows):
        part = factors[0, rows].astype(jnp.float32) * factors[1, rows].astype(jnp.float32)
        product[rows] = part.astype(jnp.bfloat16)

    def start_far(first, last):
        for n in order[first:last]:
            far_copy(piece_of(n), n).start()

    def start_near(first, last):
        for n in order[first:last]:
            near_copy(piece_of(n), n).start()

    half_rows = EARLY * PIECE
    multiply(slice(0, half_rows))
    multiply(carried_rows)
    pl.semaphore_wait(barrier, receivers)

    @pl.when(jnp.logical_and(odd == 1, has_high))
    def _():
        far_copy(piece_of(0), 0).start()
        lift_copy().start()
        start_far(1, EARLY)

    @pl.when(carries)
    def _():
        for n in range(EARLY):
            far_copy(piece_of(n), n).start()
            near_copy(piece_of(n), n).start()

    @pl.when(jnp.logical_and(even, jnp.logical_not(has_high)))
    def _():
        start_near(0, EARLY)

    multiply(slice(half_rows, channels - 2 * CHUNK))
    multiply(slice(channels - CHUNK, channels))

    @pl.when(jnp.logical_and(odd == 1, has_high))
    def _():
        start_far(EARLY, pieces)

    @pl.when(even)
    def _():
        start_near(EARLY, pieces)

    load_query.start()
    load_weight(0).start()
    weight_copy.start()
    for copy in small:
        copy.wait()

    @pl.when(jnp.logical_not(has_low))
    def _():
        back[0] = jnp.zeros_like(back[0])

    @pl.when(me == 0)
    def _():
        back[1] = jnp.zeros_like(back[1])

    freqs = in_ref.shape[0] // 2
    hidden_count = in_ref.shape[1]
    lag = lax.broadcasted_iota(jnp.int32, (freqs, lags), 1)
    seeds = as_column(seed_ref[...].astype(jnp.float32), freqs).astype(jnp.int32)
    angles = ((seeds * lag) & (seq_len - 1)).astype(jnp.float32) * (2.0 * math.pi / seq_len)
    features = jnp.concatenate([jnp.cos(angles), jnp.sin(angles)], axis=0)
    first_dims = (((0,), (0,)), ((), ()))
    hidden = jnp.sin(
        lax.dot_general(
            in_ref[...],
            features,
            first_dims,
            precision=lax.Precision.HIGHEST,
            preferred_element_type=jnp.float32,
        )
        + as_column(bias_ref[...], hidden_count)
    )
    shaped = lax.dot_general(
        fout_ref[...],
        hidden,
        first_dims,
        precision=lax.Precision.HIGHEST,
        preferred_element_type=jnp.float32,
    )
    lag = lax.broadcasted_iota(jnp.int32, (filters, lags), 1).astype(jnp.float32)
    envelope = jnp.exp(-as_column(decay_ref[...], filters) * lag) * (1.0 / math.sqrt(lags))
    inside = lag < as_column(reach_ref[...].astype(jnp.float32), filters) * block
    taps[...] = (
        jnp.where(inside, shaped * envelope, 0.0).astype(jnp.bfloat16).astype(jnp.float32)
    )

    total[...] = jnp.zeros_like(total)
    load_query.wait()
    source_tok = lax.broadcasted_iota(jnp.int32, (block, block), 0)
    target_tok = lax.broadcasted_iota(jnp.int32, (block, block), 1)
    upper = target_tok >= source_tok

    def spread(row):
        return pltpu.roll(
            jnp.broadcast_to(row, (block, block)), 0, 1, stride=1, stride_axis=0
        ).astype(jnp.bfloat16)

    def band(group):
        tap_row = taps[pl.ds(group, 1), :]
        low = spread(tap_row[:, :block])
        high = spread(tap_row[:, block:])
        zero = jnp.zeros_like(low)
        return (
            jnp.where(upper, zero, high),
            jnp.where(upper, high, low),
            jnp.where(upper, low, zero),
        )

    def skip_rows(n):
        return jnp.broadcast_to(skip_ref[pl.ds(n, 1), :], (PIECE, PIECE)).T

    for n in range(halves):
        skip_wide[n * PIECE : (n + 1) * PIECE, :] = skip_rows(whole + n)
    for j in range(CHUNK // per_group):
        for i, part in enumerate(band(whole * groups_piece + j)):
            toeplitz[j, i * block : (i + 1) * block] = part

    @pl.when(carries)
    def _():
        lift_copy().wait_recv()
        for i in range(halves):
            carry_copy(i).start()
        for n in range(EARLY, pieces):
            far_copy(piece_of(n), n).start()

    def wait_both(n):
        both = back.at[:, piece_of(n)]
        pltpu.make_async_copy(both, both, arrive_sem.at[n]).wait()

    def wait_first(n):
        @pl.when(me == 1)
        def _():
            near_copy(piece_of(n), n).wait_recv()

    def arrive(n):
        pl.when(has_low)(lambda: wait_both(n))
        wait_first(n)

        @pl.when(jnp.logical_and(relays, n < carried[0]))
        def _():
            relay_copy(piece_of(n), n).start()

    def gate(row, matrix, skip):
        rows = pl.ds(pl.multiple_of(row, per_group), per_group)
        own = product[rows, :]
        window = jnp.concatenate([back[0, rows, :], back[1, rows, :], own], axis=1)
        mixed = jnp.dot(window, matrix, preferred_element_type=jnp.float32)
        mixed = mixed + skip * own.astype(jnp.float32)
        return (query[rows, :].astype(jnp.float32) * mixed).astype(jnp.bfloat16)

    @pl.loop(0, chunks - 1)
    def _(k):
        load_weight(k + 1).start()

        @pl.when(jnp.logical_and(relays, k == chunks - 2))
        def _():
            for n in range(whole, pieces):
                wait_both(n)
                relay_copy(piece_of(n), n).start()

        for half in range(halves):
            n = k * halves + half
            arrive(n)
            skip = skip_rows(n)
            for j in range(groups_piece):
                start = j * per_group
                matrix = jnp.concatenate(band(n * groups_piece + j), axis=0)
                place = half * PIECE + start
                gated[place : place + per_group, :] = gate(
                    n * PIECE + start, matrix, skip[start : start + per_group]
                )
        load_weight(k).wait()
        chunk = gated[...].T
        for half in range(2):
            total[half] += jnp.dot(
                chunk,
                weight[rows_of(k), half * cols : (half + 1) * cols],
                preferred_element_type=jnp.float32,
            )

    part_out[...] = total[other].astype(jnp.bfloat16)
    part_copy.start()
    load_weight(chunks - 1).wait()
    for i, (offset, size) in enumerate(tail):
        pl.when(jnp.logical_and(has_low, even))(lambda: wait_both(whole + i))
        wait_first(whole + i)
        for row in range(offset, offset + size, per_group):
            place = row - (channels - CHUNK)
            gated_tail[0, place : place + per_group, :] = gate(
                row, toeplitz[place // per_group], skip_wide[place : place + per_group, :]
            )
        place = offset - (channels - CHUNK)
        gated_copy(slice(place, place + size), min(i, 1)).start()

    part_copy.wait_recv()
    total[core] += part_in[...].astype(jnp.float32) + jnp.dot(
        gated_tail[0].T, weight[last_rows, half_cols(core)], preferred_element_type=jnp.float32
    )
    weight_copy.wait_recv()
    first_tail = slice(0, tail[0][1])
    rest_tail = slice(tail[0][1], CHUNK)
    gated_copy(first_tail, 0).wait_recv()
    total[core] += jnp.dot(
        gated_tail[1, first_tail].T, weight_in[first_tail], preferred_element_type=jnp.float32
    )

    everything = slice(0, channels)

    @pl.when(has_high)
    def _():
        far_copy(everything, 0).wait_send()

    @pl.when(even)
    def _():
        near_copy(everything, 0).wait_send()

    @pl.when(relays)
    def _():
        relay_copy(slice(0, channels - CHUNK), 0).wait_send()

    @pl.when(has_high)
    def _():
        lift_copy().wait_send()

    weight_copy.wait_send()
    part_copy.wait_send()
    gated_copy(slice(0, CHUNK), 0).wait_send()
    gated_copy(rest_tail, 1).wait_recv()
    out_ref[...] = (
        total[core]
        + jnp.dot(gated_tail[1, rest_tail].T, weight_in[rest_tail], preferred_element_type=jnp.float32)
    ).astype(jnp.bfloat16)


def piece_tail(channels):
    start = channels - CHUNK
    sizes = [PIECE] + [LAST] * ((CHUNK - PIECE) // LAST)
    return [(start + sum(sizes[:i]), size) for i, size in enumerate(sizes)]


def halo_body(
    query_feat,
    key_feat,
    value_feat,
    filter_seed,
    filter_in,
    filter_bias,
    filter_out,
    decay_rate,
    reach_blocks,
    skip_gain,
    out_weight,
):
    channels, block = query_feat.shape
    seq_count = lax.axis_size("seq")
    filters = decay_rate.shape[0]
    cols = out_weight.shape[1] // 2
    pieces = (channels - CHUNK) // PIECE + len(piece_tail(channels))
    small = (
        filter_seed.reshape(1, -1),
        filter_in,
        filter_bias.reshape(1, -1),
        filter_out,
        decay_rate.reshape(1, -1),
        reach_blocks.reshape(1, -1),
        skip_gain.reshape(-1, 128),
    )
    lags = block * 2
    return pl.pallas_call(
        functools.partial(halo_kernel, seq_count),
        out_shape=pltpu.VMEM((block, cols), jnp.bfloat16),
        in_specs=[pl.BlockSpec(memory_space=pltpu.HBM)] * 11,
        out_specs=pl.BlockSpec(memory_space=pltpu.VMEM),
        scratch_shapes=[
            *[pltpu.VMEM(array.shape, array.dtype) for array in small],
            pltpu.VMEM((channels, block), jnp.bfloat16),
            pltpu.VMEM((2, channels, block), jnp.bfloat16),
            pltpu.VMEM(out_weight.shape, jnp.bfloat16),
            pltpu.VMEM((channels, block), jnp.bfloat16),
            pltpu.VMEM((2, channels, block), jnp.bfloat16),
            pltpu.VMEM((CHUNK, block), jnp.bfloat16),
            pltpu.VMEM((filters, lags), jnp.float32),
            pltpu.VMEM((CHUNK * filters // channels, 3 * block, block), jnp.bfloat16),
            pltpu.VMEM((CHUNK, block), jnp.float32),
            pltpu.VMEM((CHUNK, block), jnp.bfloat16),
            pltpu.VMEM((2, CHUNK, block), jnp.bfloat16),
            pltpu.VMEM((CHUNK, cols), jnp.bfloat16),
            pltpu.VMEM((2, block, cols), jnp.float32),
            pltpu.VMEM((block, cols), jnp.bfloat16),
            pltpu.VMEM((block, cols), jnp.bfloat16),
            pltpu.SemaphoreType.DMA((len(small),)),
            pltpu.SemaphoreType.DMA,
            pltpu.SemaphoreType.DMA,
            pltpu.SemaphoreType.DMA((2,)),
            pltpu.SemaphoreType.DMA((3,)),
            pltpu.SemaphoreType.DMA((pieces,)),
            pltpu.SemaphoreType.DMA,
            pltpu.SemaphoreType.DMA((3,)),
            pltpu.SemaphoreType.DMA((4,)),
        ],
        compiler_params=pltpu.CompilerParams(
            collective_id=0, has_side_effects=True, vmem_limit_bytes=32 * 2**20
        ),
        name="halo_conv_project",
    )(
        *(
            pltpu.with_memory_space_constraint(array, pltpu.HBM)
            for array in (query_feat, key_feat, value_feat, *small, out_weight)
        )
    )


def filter_rows(
    lag_index,
    filter_seed,
    filter_in,
    filter_bias,
    filter_out,
    decay_rate,
    reach_blocks,
    block_len,
    seq_len,
    reach_max,
):
    safe_lag = jnp.maximum(lag_index, 0)
    phases = safe_lag[:, None] * filter_seed[None, :] % seq_len
    angles = phases.astype(jnp.float32) * (2.0 * math.pi / seq_len)
    features = jnp.concatenate([jnp.cos(angles), jnp.sin(angles)], axis=1)
    hidden = jnp.sin(
        jnp.dot(
            features, filter_in, precision=lax.Precision.HIGHEST, preferred_element_type=jnp.float32
        )
        + filter_bias
    )
    shaped = jnp.dot(
        hidden, filter_out, precision=lax.Precision.HIGHEST, preferred_element_type=jnp.float32
    )
    envelope = jnp.exp(-decay_rate[None, :] * safe_lag.astype(jnp.float32)[:, None]) * (
        1.0 / math.sqrt(reach_max * block_len)
    )
    inside = (lag_index[:, None] >= 0) & (lag_index[:, None] < reach_blocks[None, :] * block_len)
    return jnp.where(inside, shaped * envelope, 0.0).astype(jnp.bfloat16)


def hankel_rows(tap_rows, sub_len, span_len):
    return jnp.stack(
        [
            tap_rows[:, sub_len - 1 - offset : sub_len - 1 - offset + span_len]
            for offset in range(sub_len)
        ],
        axis=1,
    )


def body(
    query_feat,
    key_feat,
    value_feat,
    filter_seed,
    filter_in,
    filter_bias,
    filter_out,
    decay_rate,
    reach_blocks,
    skip_gain,
    out_weight,
):
    channels, block = query_feat.shape
    seq_count = lax.axis_size("seq")
    reach_max = seq_count // 4
    seq_len = block * seq_count
    sub_len = min(128, block)
    span_len = reach_max * block + sub_len
    rev_len = span_len + sub_len - 1
    filter_count = decay_rate.shape[0]
    per_group = channels // filter_count
    product = (key_feat.astype(jnp.float32) * value_feat.astype(jnp.float32)).astype(jnp.bfloat16)
    lag_index = reach_max * block + sub_len - 1 - lax.iota(jnp.int32, rev_len)
    taps = filter_rows(
        lag_index,
        filter_seed,
        filter_in,
        filter_bias,
        filter_out,
        decay_rate,
        reach_blocks,
        block,
        seq_len,
        reach_max,
    ).T
    seq_index = lax.axis_index("seq")
    spread, query_all = (
        lax.all_to_all(product, "seq", split_axis=0, concat_axis=1, tiled=True),
        lax.all_to_all(query_feat, "seq", split_axis=0, concat_axis=1, tiled=True),
    )
    chan_dev = spread.shape[0]
    full_len = spread.shape[1]
    padded = jnp.concatenate(
        [jnp.zeros((chan_dev, reach_max * block), jnp.bfloat16), spread], axis=1
    )
    pieces = padded.reshape(chan_dev, -1, sub_len)
    count_tiles = full_len // sub_len
    span_blocks = span_len // sub_len
    windows = jnp.concatenate([pieces[:, k : k + count_tiles] for k in range(span_blocks)], axis=2)
    first_chan = seq_index * chan_dev
    group_ids = (first_chan + lax.iota(jnp.int32, chan_dev)) // per_group
    chan_taps = jnp.take(taps, group_ids, axis=0)
    chan_block = math.gcd(8, chan_dev)
    windows = windows.reshape(chan_dev // chan_block, chan_block, count_tiles, span_len)
    chan_taps = chan_taps.reshape(chan_dev // chan_block, chan_block, rev_len)

    def convolve_chan(inputs_pair):
        window_part, tap_part = inputs_pair
        hankel = hankel_rows(tap_part, sub_len, span_len)
        return jnp.einsum("ctw,caw->cta", window_part, hankel, preferred_element_type=jnp.float32)

    convolved = lax.map(convolve_chan, (windows, chan_taps))
    convolved = convolved.reshape(chan_dev, full_len)
    skip_part = lax.dynamic_slice_in_dim(skip_gain, first_chan, chan_dev)
    mixed_part = convolved + skip_part[:, None] * spread.astype(jnp.float32)
    gated_part = (query_all.astype(jnp.float32) * mixed_part).astype(jnp.bfloat16)
    gated = lax.all_to_all(gated_part, "seq", split_axis=1, concat_axis=0, tiled=True)
    reduced = lax.psum_scatter(
        lax.dot_general(
            out_weight, gated, (((0,), (0,)), ((), ())), preferred_element_type=jnp.float32
        ),
        "chan",
        scatter_dimension=0,
        tiled=True,
    )
    return reduced.T.astype(jnp.bfloat16)


def solution(mesh):
    halo = mesh.shape["seq"] // 4 == 2 and mesh.shape["chan"] == 2
    return jax.shard_map(
        halo_body if halo else body,
        mesh=mesh,
        in_specs=(
            P("chan", ("groups", "seq")),
            P("chan", ("groups", "seq")),
            P("chan", ("groups", "seq")),
            P(),
            P(),
            P(),
            P(None, "chan"),
            P("chan"),
            P("chan"),
            P("chan"),
            P("chan", None),
        ),
        out_specs=P(("groups", "seq"), "chan"),
        check_vma=False,
    )
```

```python
import functools
import math

import jax
import jax.numpy as jnp
from jax import lax
from jax.experimental import pallas as pl
from jax.experimental.pallas import tpu as pltpu
from jax.sharding import PartitionSpec as P

MESH = pl.DeviceIdType.MESH
CHUNK = 256
PIECE = 128
LAST = 64
EARLY = 8
READY = 3


def as_column(row, size):
    rows = lax.broadcasted_iota(jnp.int32, (size, size), 0)
    cols = lax.broadcasted_iota(jnp.int32, (size, size), 1)
    spread = jnp.broadcast_to(row, (size, size))
    return jnp.sum(jnp.where(rows == cols, spread, 0.0), axis=1, keepdims=True)


def halo_kernel(
    seq_count,
    query_hbm,
    key_hbm,
    value_hbm,
    seed_hbm,
    in_hbm,
    bias_hbm,
    fout_hbm,
    decay_hbm,
    reach_hbm,
    skip_hbm,
    weight_hbm,
    out_ref,
    seed_ref,
    in_ref,
    bias_ref,
    fout_ref,
    decay_ref,
    reach_ref,
    skip_ref,
    query,
    factors,
    weight,
    product,
    back,
    lifted,
    taps,
    toeplitz,
    skip_wide,
    gated,
    gated_tail,
    weight_in,
    total,
    part_out,
    part_in,
    small_sem,
    factor_sem,
    query_sem,
    weight_sem,
    send_sem,
    arrive_sem,
    lift_sem,
    core_send,
    core_recv,
):
    channels, block = product.shape
    filters = taps.shape[0]
    per_group = channels // filters
    lags = taps.shape[1]
    chunks = channels // CHUNK
    halves = CHUNK // PIECE
    groups_piece = PIECE // per_group
    cols = out_ref.shape[1]
    seq_len = seq_count * block
    whole = (channels - CHUNK) // PIECE
    tail = piece_tail(channels)
    pieces = whole + len(tail)
    carried = list(range(whole - halves, whole))
    carried_rows = slice(channels - 2 * CHUNK, channels - CHUNK)
    order = [n for n in range(pieces) if n not in carried] + carried

    me = lax.axis_index("seq")
    core = lax.axis_index("chan")
    pair = me // 2
    odd = me % 2
    mate = me + 1 - 2 * odd
    other = 1 - core
    has_low = pair > 0
    has_high = pair < seq_count // 2 - 1
    even = odd == 0
    relays = jnp.logical_and(has_low, odd == 1)
    carries = jnp.logical_and(has_high, even)

    barrier = pltpu.get_barrier_semaphore()

    def greet(device):
        pl.semaphore_signal(barrier, inc=1, device_id=device, device_id_type=MESH)

    greet({"chan": other})
    greet({"seq": mate})
    pl.when(has_low)(lambda: greet({"seq": me - 2}))
    receivers = 2 + has_high.astype(jnp.int32)

    def rows_of(k):
        return pl.ds(pl.multiple_of(k * CHUNK, CHUNK), CHUNK)

    def piece_of(n):
        if isinstance(n, int) and n >= whole:
            return pl.ds(*tail[n - whole])
        return pl.ds(pl.multiple_of(n * PIECE, PIECE), PIECE)

    def load_weight(k):
        return pltpu.make_async_copy(
            weight_hbm.at[rows_of(k)], weight.at[rows_of(k)], weight_sem.at[k % 2]
        )

    load_key = pltpu.make_async_copy(key_hbm, factors.at[0], factor_sem)
    load_value = pltpu.make_async_copy(value_hbm, factors.at[1], factor_sem)
    load_query = pltpu.make_async_copy(query_hbm, query, query_sem)

    def far_copy(rows, n):
        return pltpu.make_async_remote_copy(
            src_ref=product.at[rows],
            dst_ref=back.at[0, rows],
            send_sem=send_sem.at[0],
            recv_sem=arrive_sem.at[n],
            device_id={"seq": me + 2},
            device_id_type=MESH,
        )

    def near_copy(rows, n):
        return pltpu.make_async_remote_copy(
            src_ref=product.at[rows],
            dst_ref=back.at[1, rows],
            send_sem=send_sem.at[1],
            recv_sem=arrive_sem.at[n],
            device_id={"seq": mate},
            device_id_type=MESH,
        )

    def relay_copy(rows, n):
        return pltpu.make_async_remote_copy(
            src_ref=back.at[0, rows],
            dst_ref=back.at[1, rows],
            send_sem=send_sem.at[1],
            recv_sem=arrive_sem.at[n],
            device_id={"seq": mate},
            device_id_type=MESH,
        )

    def lift_copy():
        return pltpu.make_async_remote_copy(
            src_ref=product.at[carried_rows],
            dst_ref=lifted,
            send_sem=send_sem.at[2],
            recv_sem=lift_sem,
            device_id={"seq": mate},
            device_id_type=MESH,
        )

    def carry_copy(i):
        return pltpu.make_async_remote_copy(
            src_ref=lifted.at[pl.ds(i * PIECE, PIECE)],
            dst_ref=back.at[1, piece_of(carried[i])],
            send_sem=send_sem.at[2],
            recv_sem=arrive_sem.at[carried[i]],
            device_id={"seq": me + 2},
            device_id_type=MESH,
        )

    last_rows = slice(channels - CHUNK, channels)

    def half_cols(half):
        return pl.ds(pl.multiple_of(half * cols, cols), cols)

    weight_copy = pltpu.make_async_remote_copy(
        src_ref=weight_hbm.at[last_rows, half_cols(other)],
        dst_ref=weight_in,
        send_sem=core_send.at[0],
        recv_sem=core_recv.at[0],
        device_id={"chan": other},
        device_id_type=MESH,
    )
    part_copy = pltpu.make_async_remote_copy(
        src_ref=part_out,
        dst_ref=part_in,
        send_sem=core_send.at[1],
        recv_sem=core_recv.at[1],
        device_id={"chan": other},
        device_id_type=MESH,
    )

    def gated_copy(rows, i):
        return pltpu.make_async_remote_copy(
            src_ref=gated_tail.at[0, rows],
            dst_ref=gated_tail.at[1, rows],
            send_sem=core_send.at[2],
            recv_sem=core_recv.at[2 + i],
            device_id={"chan": other},
            device_id_type=MESH,
        )

    load_key.start()
    load_value.start()
    small = [
        pltpu.make_async_copy(source, target, small_sem.at[i])
        for i, (source, target) in enumerate(
            (
                (seed_hbm, seed_ref),
                (in_hbm, in_ref),
                (bias_hbm, bias_ref),
                (fout_hbm, fout_ref),
                (decay_hbm, decay_ref),
                (reach_hbm, reach_ref),
                (skip_hbm, skip_ref),
            )
        )
    ]
    for copy in small:
        copy.start()

    pltpu.make_async_copy(factors, factors, factor_sem).wait()

    def multiply(rows):
        part = factors[0, rows].astype(jnp.float32) * factors[1, rows].astype(jnp.float32)
        product[rows] = part.astype(jnp.bfloat16)

    def start_far(first, last):
        for n in order[first:last]:
            far_copy(piece_of(n), n).start()

    def start_near(first, last):
        for n in order[first:last]:
            near_copy(piece_of(n), n).start()

    half_rows = EARLY * PIECE
    multiply(slice(0, half_rows))
    multiply(carried_rows)
    pl.semaphore_wait(barrier, receivers)

    @pl.when(jnp.logical_and(odd == 1, has_high))
    def _():
        far_copy(piece_of(0), 0).start()
        lift_copy().start()
        start_far(1, EARLY)

    @pl.when(carries)
    def _():
        for n in range(EARLY):
            far_copy(piece_of(n), n).start()
            near_copy(piece_of(n), n).start()

    @pl.when(jnp.logical_and(even, jnp.logical_not(has_high)))
    def _():
        start_near(0, EARLY)

    multiply(slice(half_rows, channels - 2 * CHUNK))
    multiply(slice(channels - CHUNK, channels))

    @pl.when(jnp.logical_and(odd == 1, has_high))
    def _():
        start_far(EARLY, pieces)

    @pl.when(even)
    def _():
        start_near(EARLY, pieces)

    load_query.start()
    load_weight(0).start()
    weight_copy.start()
    for copy in small:
        copy.wait()

    @pl.when(jnp.logical_not(has_low))
    def _():
        back[0] = jnp.zeros_like(back[0])

    @pl.when(me == 0)
    def _():
        back[1] = jnp.zeros_like(back[1])

    freqs = in_ref.shape[0] // 2
    hidden_count = in_ref.shape[1]
    lag = lax.broadcasted_iota(jnp.int32, (freqs, lags), 1)
    seeds = as_column(seed_ref[...].astype(jnp.float32), freqs).astype(jnp.int32)
    angles = ((seeds * lag) & (seq_len - 1)).astype(jnp.float32) * (2.0 * math.pi / seq_len)
    features = jnp.concatenate([jnp.cos(angles), jnp.sin(angles)], axis=0)
    first_dims = (((0,), (0,)), ((), ()))
    hidden = jnp.sin(
        lax.dot_general(
            in_ref[...],
            features,
            first_dims,
            precision=lax.Precision.HIGHEST,
            preferred_element_type=jnp.float32,
        )
        + as_column(bias_ref[...], hidden_count)
    )
    shaped = lax.dot_general(
        fout_ref[...],
        hidden,
        first_dims,
        precision=lax.Precision.HIGHEST,
        preferred_element_type=jnp.float32,
    )
    lag = lax.broadcasted_iota(jnp.int32, (filters, lags), 1).astype(jnp.float32)
    envelope = jnp.exp(-as_column(decay_ref[...], filters) * lag) * (1.0 / math.sqrt(lags))
    inside = lag < as_column(reach_ref[...].astype(jnp.float32), filters) * block
    taps[...] = (
        jnp.where(inside, shaped * envelope, 0.0).astype(jnp.bfloat16).astype(jnp.float32)
    )

    total[...] = jnp.zeros_like(total)
    load_query.wait()
    source_tok = lax.broadcasted_iota(jnp.int32, (block, block), 0)
    target_tok = lax.broadcasted_iota(jnp.int32, (block, block), 1)
    upper = target_tok >= source_tok

    def spread(row):
        return pltpu.roll(
            jnp.broadcast_to(row, (block, block)), 0, 1, stride=1, stride_axis=0
        ).astype(jnp.bfloat16)

    def band(group):
        tap_row = taps[pl.ds(group, 1), :]
        low = spread(tap_row[:, :block])
        high = spread(tap_row[:, block:])
        zero = jnp.zeros_like(low)
        return (
            jnp.where(upper, zero, high),
            jnp.where(upper, high, low),
            jnp.where(upper, low, zero),
        )

    def skip_rows(n):
        return jnp.broadcast_to(skip_ref[pl.ds(n, 1), :], (PIECE, PIECE)).T

    for n in range(halves):
        skip_wide[n * PIECE : (n + 1) * PIECE, :] = skip_rows(whole + n)
    first_ready = READY * CHUNK // per_group
    tail_ready = (channels - CHUNK) // per_group - first_ready

    def make_ready(slot):
        for i, part in enumerate(band(first_ready + slot)):
            toeplitz[slot, i * block : (i + 1) * block] = part

    for j in range(CHUNK // per_group):
        make_ready(tail_ready + j)

    @pl.when(carries)
    def _():
        lift_copy().wait_recv()
        for i in range(halves):
            carry_copy(i).start()
        for n in range(EARLY, pieces):
            far_copy(piece_of(n), n).start()

    @pl.when(even)
    def _():
        @pl.loop(0, tail_ready // groups_piece)
        def _(i):
            for j in range(groups_piece):
                make_ready(i * groups_piece + j)

    def wait_both(n):
        both = back.at[:, piece_of(n)]
        pltpu.make_async_copy(both, both, arrive_sem.at[n]).wait()

    def wait_first(n):
        @pl.when(me == 1)
        def _():
            near_copy(piece_of(n), n).wait_recv()

    def arrive(n):
        pl.when(has_low)(lambda: wait_both(n))
        wait_first(n)

        @pl.when(jnp.logical_and(relays, n < carried[0]))
        def _():
            relay_copy(piece_of(n), n).start()

    def gate(row, matrix, skip):
        rows = pl.ds(pl.multiple_of(row, per_group), per_group)
        own = product[rows, :]
        window = jnp.concatenate([back[0, rows, :], back[1, rows, :], own], axis=1)
        mixed = jnp.dot(window, matrix, preferred_element_type=jnp.float32)
        mixed = mixed + skip * own.astype(jnp.float32)
        return (query[rows, :].astype(jnp.float32) * mixed).astype(jnp.bfloat16)

    @pl.loop(0, chunks - 1)
    def _(k):
        load_weight(k + 1).start()

        @pl.when(jnp.logical_and(relays, k == chunks - 2))
        def _():
            for n in range(whole, pieces):
                wait_both(n)
                relay_copy(piece_of(n), n).start()

        for half in range(halves):
            n = k * halves + half
            arrive(n)
            ready = jnp.logical_and(even, k >= READY)

            def convolve(matrix_of):
                skip = skip_rows(n)
                for j in range(groups_piece):
                    start = j * per_group
                    place = half * PIECE + start
                    gated[place : place + per_group, :] = gate(
                        n * PIECE + start,
                        matrix_of(n * groups_piece + j),
                        skip[start : start + per_group],
                    )

            @pl.when(ready)
            def _():
                convolve(lambda group: toeplitz[group - first_ready])

            @pl.when(jnp.logical_not(ready))
            def _():
                convolve(lambda group: jnp.concatenate(band(group), axis=0))

        load_weight(k).wait()
        chunk = gated[...].T
        for half in range(2):
            total[half] += jnp.dot(
                chunk,
                weight[rows_of(k), half * cols : (half + 1) * cols],
                preferred_element_type=jnp.float32,
            )

    part_out[...] = total[other].astype(jnp.bfloat16)
    part_copy.start()
    load_weight(chunks - 1).wait()
    for i, (offset, size) in enumerate(tail):
        pl.when(jnp.logical_and(has_low, even))(lambda: wait_both(whole + i))
        wait_first(whole + i)
        for row in range(offset, offset + size, per_group):
            place = row - (channels - CHUNK)
            gated_tail[0, place : place + per_group, :] = gate(
                row, toeplitz[tail_ready + place // per_group], skip_wide[place : place + per_group, :]
            )
        place = offset - (channels - CHUNK)
        gated_copy(slice(place, place + size), min(i, 1)).start()

    part_copy.wait_recv()
    total[core] += part_in[...].astype(jnp.float32) + jnp.dot(
        gated_tail[0].T, weight[last_rows, half_cols(core)], preferred_element_type=jnp.float32
    )
    weight_copy.wait_recv()
    first_tail = slice(0, tail[0][1])
    rest_tail = slice(tail[0][1], CHUNK)
    gated_copy(first_tail, 0).wait_recv()
    total[core] += jnp.dot(
        gated_tail[1, first_tail].T, weight_in[first_tail], preferred_element_type=jnp.float32
    )

    everything = slice(0, channels)

    @pl.when(has_high)
    def _():
        far_copy(everything, 0).wait_send()

    @pl.when(even)
    def _():
        near_copy(everything, 0).wait_send()

    @pl.when(relays)
    def _():
        relay_copy(slice(0, channels - CHUNK), 0).wait_send()

    @pl.when(has_high)
    def _():
        lift_copy().wait_send()

    weight_copy.wait_send()
    part_copy.wait_send()
    gated_copy(slice(0, CHUNK), 0).wait_send()
    gated_copy(rest_tail, 1).wait_recv()
    out_ref[...] = (
        total[core]
        + jnp.dot(gated_tail[1, rest_tail].T, weight_in[rest_tail], preferred_element_type=jnp.float32)
    ).astype(jnp.bfloat16)


def piece_tail(channels):
    start = channels - CHUNK
    sizes = [PIECE] + [LAST] * ((CHUNK - PIECE) // LAST)
    return [(start + sum(sizes[:i]), size) for i, size in enumerate(sizes)]


def halo_body(
    query_feat,
    key_feat,
    value_feat,
    filter_seed,
    filter_in,
    filter_bias,
    filter_out,
    decay_rate,
    reach_blocks,
    skip_gain,
    out_weight,
):
    channels, block = query_feat.shape
    seq_count = lax.axis_size("seq")
    filters = decay_rate.shape[0]
    cols = out_weight.shape[1] // 2
    pieces = (channels - CHUNK) // PIECE + len(piece_tail(channels))
    small = (
        filter_seed.reshape(1, -1),
        filter_in,
        filter_bias.reshape(1, -1),
        filter_out,
        decay_rate.reshape(1, -1),
        reach_blocks.reshape(1, -1),
        skip_gain.reshape(-1, 128),
    )
    lags = block * 2
    return pl.pallas_call(
        functools.partial(halo_kernel, seq_count),
        out_shape=pltpu.VMEM((block, cols), jnp.bfloat16),
        in_specs=[pl.BlockSpec(memory_space=pltpu.HBM)] * 11,
        out_specs=pl.BlockSpec(memory_space=pltpu.VMEM),
        scratch_shapes=[
            *[pltpu.VMEM(array.shape, array.dtype) for array in small],
            pltpu.VMEM((channels, block), jnp.bfloat16),
            pltpu.VMEM((2, channels, block), jnp.bfloat16),
            pltpu.VMEM(out_weight.shape, jnp.bfloat16),
            pltpu.VMEM((channels, block), jnp.bfloat16),
            pltpu.VMEM((2, channels, block), jnp.bfloat16),
            pltpu.VMEM((CHUNK, block), jnp.bfloat16),
            pltpu.VMEM((filters, lags), jnp.float32),
            pltpu.VMEM(
                ((channels - READY * CHUNK) * filters // channels, 3 * block, block), jnp.bfloat16
            ),
            pltpu.VMEM((CHUNK, block), jnp.float32),
            pltpu.VMEM((CHUNK, block), jnp.bfloat16),
            pltpu.VMEM((2, CHUNK, block), jnp.bfloat16),
            pltpu.VMEM((CHUNK, cols), jnp.bfloat16),
            pltpu.VMEM((2, block, cols), jnp.float32),
            pltpu.VMEM((block, cols), jnp.bfloat16),
            pltpu.VMEM((block, cols), jnp.bfloat16),
            pltpu.SemaphoreType.DMA((len(small),)),
            pltpu.SemaphoreType.DMA,
            pltpu.SemaphoreType.DMA,
            pltpu.SemaphoreType.DMA((2,)),
            pltpu.SemaphoreType.DMA((3,)),
            pltpu.SemaphoreType.DMA((pieces,)),
            pltpu.SemaphoreType.DMA,
            pltpu.SemaphoreType.DMA((3,)),
            pltpu.SemaphoreType.DMA((4,)),
        ],
        compiler_params=pltpu.CompilerParams(
            collective_id=0, has_side_effects=True, vmem_limit_bytes=32 * 2**20
        ),
        name="halo_conv_project",
    )(
        *(
            pltpu.with_memory_space_constraint(array, pltpu.HBM)
            for array in (query_feat, key_feat, value_feat, *small, out_weight)
        )
    )


def filter_rows(
    lag_index,
    filter_seed,
    filter_in,
    filter_bias,
    filter_out,
    decay_rate,
    reach_blocks,
    block_len,
    seq_len,
    reach_max,
):
    safe_lag = jnp.maximum(lag_index, 0)
    phases = safe_lag[:, None] * filter_seed[None, :] % seq_len
    angles = phases.astype(jnp.float32) * (2.0 * math.pi / seq_len)
    features = jnp.concatenate([jnp.cos(angles), jnp.sin(angles)], axis=1)
    hidden = jnp.sin(
        jnp.dot(
            features, filter_in, precision=lax.Precision.HIGHEST, preferred_element_type=jnp.float32
        )
        + filter_bias
    )
    shaped = jnp.dot(
        hidden, filter_out, precision=lax.Precision.HIGHEST, preferred_element_type=jnp.float32
    )
    envelope = jnp.exp(-decay_rate[None, :] * safe_lag.astype(jnp.float32)[:, None]) * (
        1.0 / math.sqrt(reach_max * block_len)
    )
    inside = (lag_index[:, None] >= 0) & (lag_index[:, None] < reach_blocks[None, :] * block_len)
    return jnp.where(inside, shaped * envelope, 0.0).astype(jnp.bfloat16)


def hankel_rows(tap_rows, sub_len, span_len):
    return jnp.stack(
        [
            tap_rows[:, sub_len - 1 - offset : sub_len - 1 - offset + span_len]
            for offset in range(sub_len)
        ],
        axis=1,
    )


def body(
    query_feat,
    key_feat,
    value_feat,
    filter_seed,
    filter_in,
    filter_bias,
    filter_out,
    decay_rate,
    reach_blocks,
    skip_gain,
    out_weight,
):
    channels, block = query_feat.shape
    seq_count = lax.axis_size("seq")
    reach_max = seq_count // 4
    seq_len = block * seq_count
    sub_len = min(128, block)
    span_len = reach_max * block + sub_len
    rev_len = span_len + sub_len - 1
    filter_count = decay_rate.shape[0]
    per_group = channels // filter_count
    product = (key_feat.astype(jnp.float32) * value_feat.astype(jnp.float32)).astype(jnp.bfloat16)
    lag_index = reach_max * block + sub_len - 1 - lax.iota(jnp.int32, rev_len)
    taps = filter_rows(
        lag_index,
        filter_seed,
        filter_in,
        filter_bias,
        filter_out,
        decay_rate,
        reach_blocks,
        block,
        seq_len,
        reach_max,
    ).T
    seq_index = lax.axis_index("seq")
    spread, query_all = (
        lax.all_to_all(product, "seq", split_axis=0, concat_axis=1, tiled=True),
        lax.all_to_all(query_feat, "seq", split_axis=0, concat_axis=1, tiled=True),
    )
    chan_dev = spread.shape[0]
    full_len = spread.shape[1]
    padded = jnp.concatenate(
        [jnp.zeros((chan_dev, reach_max * block), jnp.bfloat16), spread], axis=1
    )
    pieces = padded.reshape(chan_dev, -1, sub_len)
    count_tiles = full_len // sub_len
    span_blocks = span_len // sub_len
    windows = jnp.concatenate([pieces[:, k : k + count_tiles] for k in range(span_blocks)], axis=2)
    first_chan = seq_index * chan_dev
    group_ids = (first_chan + lax.iota(jnp.int32, chan_dev)) // per_group
    chan_taps = jnp.take(taps, group_ids, axis=0)
    chan_block = math.gcd(8, chan_dev)
    windows = windows.reshape(chan_dev // chan_block, chan_block, count_tiles, span_len)
    chan_taps = chan_taps.reshape(chan_dev // chan_block, chan_block, rev_len)

    def convolve_chan(inputs_pair):
        window_part, tap_part = inputs_pair
        hankel = hankel_rows(tap_part, sub_len, span_len)
        return jnp.einsum("ctw,caw->cta", window_part, hankel, preferred_element_type=jnp.float32)

    convolved = lax.map(convolve_chan, (windows, chan_taps))
    convolved = convolved.reshape(chan_dev, full_len)
    skip_part = lax.dynamic_slice_in_dim(skip_gain, first_chan, chan_dev)
    mixed_part = convolved + skip_part[:, None] * spread.astype(jnp.float32)
    gated_part = (query_all.astype(jnp.float32) * mixed_part).astype(jnp.bfloat16)
    gated = lax.all_to_all(gated_part, "seq", split_axis=1, concat_axis=0, tiled=True)
    reduced = lax.psum_scatter(
        lax.dot_general(
            out_weight, gated, (((0,), (0,)), ((), ())), preferred_element_type=jnp.float32
        ),
        "chan",
        scatter_dimension=0,
        tiled=True,
    )
    return reduced.T.astype(jnp.bfloat16)


def solution(mesh):
    halo = mesh.shape["seq"] // 4 == 2 and mesh.shape["chan"] == 2
    return jax.shard_map(
        halo_body if halo else body,
        mesh=mesh,
        in_specs=(
            P("chan", ("groups", "seq")),
            P("chan", ("groups", "seq")),
            P("chan", ("groups", "seq")),
            P(),
            P(),
            P(),
            P(None, "chan"),
            P("chan"),
            P("chan"),
            P("chan"),
            P("chan", None),
        ),
        out_specs=P(("groups", "seq"), "chan"),
        check_vma=False,
    )
```

```python
import functools
import math

import jax
import jax.numpy as jnp
from jax import lax
from jax.experimental import pallas as pl
from jax.experimental.pallas import tpu as pltpu
from jax.sharding import PartitionSpec as P

MESH = pl.DeviceIdType.MESH
CHUNK = 256
PIECE = 128
LAST = 64
EARLY = 6
READY = 4
CARRY_AT = 5


def as_column(row, size):
    rows = lax.broadcasted_iota(jnp.int32, (size, size), 0)
    cols = lax.broadcasted_iota(jnp.int32, (size, size), 1)
    spread = jnp.broadcast_to(row, (size, size))
    return jnp.sum(jnp.where(rows == cols, spread, 0.0), axis=1, keepdims=True)


def halo_kernel(
    seq_count,
    query_hbm,
    key_hbm,
    value_hbm,
    seed_hbm,
    in_hbm,
    bias_hbm,
    fout_hbm,
    decay_hbm,
    reach_hbm,
    skip_hbm,
    weight_hbm,
    out_ref,
    seed_ref,
    in_ref,
    bias_ref,
    fout_ref,
    decay_ref,
    reach_ref,
    skip_ref,
    query,
    factors,
    weight,
    product,
    back,
    lifted,
    taps,
    toeplitz,
    skip_wide,
    gated,
    gated_tail,
    weight_in,
    total,
    part_out,
    part_in,
    small_sem,
    factor_sem,
    query_sem,
    weight_sem,
    send_sem,
    arrive_sem,
    lift_sem,
    core_send,
    core_recv,
):
    channels, block = product.shape
    filters = taps.shape[0]
    per_group = channels // filters
    lags = taps.shape[1]
    chunks = channels // CHUNK
    halves = CHUNK // PIECE
    groups_piece = PIECE // per_group
    cols = out_ref.shape[1]
    seq_len = seq_count * block
    whole = (channels - CHUNK) // PIECE
    tail = piece_tail(channels)
    pieces = whole + len(tail)
    carried = list(range(whole - halves, whole))
    carried_rows = slice(channels - 2 * CHUNK, channels - CHUNK)
    order = [n for n in range(pieces) if n not in carried] + carried

    me = lax.axis_index("seq")
    core = lax.axis_index("chan")
    pair = me // 2
    odd = me % 2
    mate = me + 1 - 2 * odd
    other = 1 - core
    has_low = pair > 0
    has_high = pair < seq_count // 2 - 1
    even = odd == 0
    relays = jnp.logical_and(has_low, odd == 1)
    carries = jnp.logical_and(has_high, even)

    barrier = pltpu.get_barrier_semaphore()

    def greet(device):
        pl.semaphore_signal(barrier, inc=1, device_id=device, device_id_type=MESH)

    greet({"chan": other})
    greet({"seq": mate})
    pl.when(has_low)(lambda: greet({"seq": me - 2}))
    receivers = 2 + has_high.astype(jnp.int32)

    def rows_of(k):
        return pl.ds(pl.multiple_of(k * CHUNK, CHUNK), CHUNK)

    def piece_of(n):
        if isinstance(n, int) and n >= whole:
            return pl.ds(*tail[n - whole])
        return pl.ds(pl.multiple_of(n * PIECE, PIECE), PIECE)

    def chunk_at(k):
        lifted_chunk = chunks - 2
        moved = jnp.where(k == CARRY_AT, lifted_chunk, jnp.where(k > CARRY_AT, k - 1, k))
        return jnp.where(jnp.logical_and(even, k <= lifted_chunk), moved, k)

    def load_weight(k):
        rows = rows_of(chunk_at(k))
        return pltpu.make_async_copy(weight_hbm.at[rows], weight.at[rows], weight_sem.at[k % 2])

    load_key = pltpu.make_async_copy(key_hbm, factors.at[0], factor_sem)
    load_value = pltpu.make_async_copy(value_hbm, factors.at[1], factor_sem)
    load_query = pltpu.make_async_copy(query_hbm, query, query_sem)

    def far_copy(rows, n):
        return pltpu.make_async_remote_copy(
            src_ref=product.at[rows],
            dst_ref=back.at[0, rows],
            send_sem=send_sem.at[0],
            recv_sem=arrive_sem.at[n],
            device_id={"seq": me + 2},
            device_id_type=MESH,
        )

    def near_copy(rows, n):
        return pltpu.make_async_remote_copy(
            src_ref=product.at[rows],
            dst_ref=back.at[1, rows],
            send_sem=send_sem.at[1],
            recv_sem=arrive_sem.at[n],
            device_id={"seq": mate},
            device_id_type=MESH,
        )

    def relay_copy(rows, n):
        return pltpu.make_async_remote_copy(
            src_ref=back.at[0, rows],
            dst_ref=back.at[1, rows],
            send_sem=send_sem.at[1],
            recv_sem=arrive_sem.at[n],
            device_id={"seq": mate},
            device_id_type=MESH,
        )

    def lift_copy():
        return pltpu.make_async_remote_copy(
            src_ref=product.at[carried_rows],
            dst_ref=lifted,
            send_sem=send_sem.at[2],
            recv_sem=lift_sem,
            device_id={"seq": mate},
            device_id_type=MESH,
        )

    def carry_copy(i):
        return pltpu.make_async_remote_copy(
            src_ref=lifted.at[pl.ds(i * PIECE, PIECE)],
            dst_ref=back.at[1, piece_of(carried[i])],
            send_sem=send_sem.at[2],
            recv_sem=arrive_sem.at[carried[i]],
            device_id={"seq": me + 2},
            device_id_type=MESH,
        )

    last_rows = slice(channels - CHUNK, channels)

    def half_cols(half):
        return pl.ds(pl.multiple_of(half * cols, cols), cols)

    weight_copy = pltpu.make_async_remote_copy(
        src_ref=weight_hbm.at[last_rows, half_cols(other)],
        dst_ref=weight_in,
        send_sem=core_send.at[0],
        recv_sem=core_recv.at[0],
        device_id={"chan": other},
        device_id_type=MESH,
    )
    part_copy = pltpu.make_async_remote_copy(
        src_ref=part_out,
        dst_ref=part_in,
        send_sem=core_send.at[1],
        recv_sem=core_recv.at[1],
        device_id={"chan": other},
        device_id_type=MESH,
    )

    def gated_copy(rows, i):
        return pltpu.make_async_remote_copy(
            src_ref=gated_tail.at[0, rows],
            dst_ref=gated_tail.at[1, rows],
            send_sem=core_send.at[2],
            recv_sem=core_recv.at[2 + i],
            device_id={"chan": other},
            device_id_type=MESH,
        )

    load_key.start()
    load_value.start()
    small = [
        pltpu.make_async_copy(source, target, small_sem.at[i])
        for i, (source, target) in enumerate(
            (
                (seed_hbm, seed_ref),
                (in_hbm, in_ref),
                (bias_hbm, bias_ref),
                (fout_hbm, fout_ref),
                (decay_hbm, decay_ref),
                (reach_hbm, reach_ref),
                (skip_hbm, skip_ref),
            )
        )
    ]
    for copy in small:
        copy.start()

    pltpu.make_async_copy(factors, factors, factor_sem).wait()

    def multiply(rows):
        part = factors[0, rows].astype(jnp.float32) * factors[1, rows].astype(jnp.float32)
        product[rows] = part.astype(jnp.bfloat16)

    def start_far(first, last):
        for n in order[first:last]:
            far_copy(piece_of(n), n).start()

    def start_near(first, last):
        for n in order[first:last]:
            near_copy(piece_of(n), n).start()

    half_rows = EARLY * PIECE
    multiply(slice(0, half_rows))
    multiply(carried_rows)
    pl.semaphore_wait(barrier, receivers)

    @pl.when(jnp.logical_and(odd == 1, has_high))
    def _():
        far_copy(piece_of(0), 0).start()
        lift_copy().start()
        start_far(1, EARLY)

    @pl.when(carries)
    def _():
        for n in range(EARLY):
            far_copy(piece_of(n), n).start()
            near_copy(piece_of(n), n).start()

    @pl.when(jnp.logical_and(even, jnp.logical_not(has_high)))
    def _():
        start_near(0, EARLY)

    multiply(slice(half_rows, channels - 2 * CHUNK))
    multiply(slice(channels - CHUNK, channels))

    @pl.when(jnp.logical_and(odd == 1, has_high))
    def _():
        start_far(EARLY, pieces)

    @pl.when(even)
    def _():
        start_near(EARLY, pieces)

    load_query.start()
    load_weight(0).start()
    weight_copy.start()
    for copy in small:
        copy.wait()

    @pl.when(jnp.logical_not(has_low))
    def _():
        back[0] = jnp.zeros_like(back[0])

    @pl.when(me == 0)
    def _():
        back[1] = jnp.zeros_like(back[1])

    freqs = in_ref.shape[0] // 2
    hidden_count = in_ref.shape[1]
    lag = lax.broadcasted_iota(jnp.int32, (freqs, lags), 1)
    seeds = as_column(seed_ref[...].astype(jnp.float32), freqs).astype(jnp.int32)
    angles = ((seeds * lag) & (seq_len - 1)).astype(jnp.float32) * (2.0 * math.pi / seq_len)
    features = jnp.concatenate([jnp.cos(angles), jnp.sin(angles)], axis=0)
    first_dims = (((0,), (0,)), ((), ()))
    hidden = jnp.sin(
        lax.dot_general(
            in_ref[...],
            features,
            first_dims,
            precision=lax.Precision.HIGHEST,
            preferred_element_type=jnp.float32,
        )
        + as_column(bias_ref[...], hidden_count)
    )
    shaped = lax.dot_general(
        fout_ref[...],
        hidden,
        first_dims,
        precision=lax.Precision.HIGHEST,
        preferred_element_type=jnp.float32,
    )
    lag = lax.broadcasted_iota(jnp.int32, (filters, lags), 1).astype(jnp.float32)
    envelope = jnp.exp(-as_column(decay_ref[...], filters) * lag) * (1.0 / math.sqrt(lags))
    inside = lag < as_column(reach_ref[...].astype(jnp.float32), filters) * block
    taps[...] = (
        jnp.where(inside, shaped * envelope, 0.0).astype(jnp.bfloat16).astype(jnp.float32)
    )

    total[...] = jnp.zeros_like(total)
    load_query.wait()
    source_tok = lax.broadcasted_iota(jnp.int32, (block, block), 0)
    target_tok = lax.broadcasted_iota(jnp.int32, (block, block), 1)
    upper = target_tok >= source_tok

    def spread(row):
        return pltpu.roll(
            jnp.broadcast_to(row, (block, block)), 0, 1, stride=1, stride_axis=0
        ).astype(jnp.bfloat16)

    def band(group):
        tap_row = taps[pl.ds(group, 1), :]
        low = spread(tap_row[:, :block])
        high = spread(tap_row[:, block:])
        zero = jnp.zeros_like(low)
        return (
            jnp.where(upper, zero, high),
            jnp.where(upper, high, low),
            jnp.where(upper, low, zero),
        )

    def skip_rows(n):
        return jnp.broadcast_to(skip_ref[pl.ds(n, 1), :], (PIECE, PIECE)).T

    for n in range(halves):
        skip_wide[n * PIECE : (n + 1) * PIECE, :] = skip_rows(whole + n)
    first_ready = READY * CHUNK // per_group
    tail_ready = (channels - CHUNK) // per_group - first_ready

    def make_ready(slot):
        for i, part in enumerate(band(first_ready + slot)):
            toeplitz[slot, i * block : (i + 1) * block] = part

    for j in range(CHUNK // per_group):
        make_ready(tail_ready + j)

    @pl.when(carries)
    def _():
        lift_copy().wait_recv()
        for i in range(halves):
            carry_copy(i).start()
        for n in range(EARLY, pieces):
            far_copy(piece_of(n), n).start()

    @pl.when(even)
    def _():
        @pl.loop(0, tail_ready // groups_piece)
        def _(i):
            for j in range(groups_piece):
                make_ready(i * groups_piece + j)

    def wait_both(n):
        both = back.at[:, piece_of(n)]
        pltpu.make_async_copy(both, both, arrive_sem.at[n]).wait()

    def wait_first(n):
        @pl.when(me == 1)
        def _():
            near_copy(piece_of(n), n).wait_recv()

    def relay(n):
        wait_both(n)
        relay_copy(piece_of(n), n).start()

    def arrive(n, first):
        ahead = jnp.logical_and(relays, n < carried[0])
        pl.when(jnp.logical_and(has_low, jnp.logical_not(ahead)))(lambda: wait_both(n))
        wait_first(n)
        if not first:
            pl.when(ahead)(lambda: relay(n))

    def gate(row, matrix, skip):
        rows = pl.ds(pl.multiple_of(row, per_group), per_group)
        own = product[rows, :]
        window = jnp.concatenate([back[0, rows, :], back[1, rows, :], own], axis=1)
        mixed = jnp.dot(window, matrix, preferred_element_type=jnp.float32)
        mixed = mixed + skip * own.astype(jnp.float32)
        return (query[rows, :].astype(jnp.float32) * mixed).astype(jnp.bfloat16)

    pl.when(relays)(lambda: relay(0))

    @pl.loop(0, chunks - 1)
    def _(k):
        load_weight(k + 1).start()

        for half in range(halves):
            n = chunk_at(k) * halves + half
            arrive(n, half == 0)
            ready = jnp.logical_and(even, k >= READY)

            def convolve(matrix_of):
                skip = skip_rows(n)
                for j in range(groups_piece):
                    start = j * per_group
                    place = half * PIECE + start
                    gated[place : place + per_group, :] = gate(
                        n * PIECE + start,
                        matrix_of(n * groups_piece + j),
                        skip[start : start + per_group],
                    )

            @pl.when(ready)
            def _():
                convolve(lambda group: toeplitz[group - first_ready])

            @pl.when(jnp.logical_not(ready))
            def _():
                convolve(lambda group: jnp.concatenate(band(group), axis=0))

        @pl.when(jnp.logical_and(relays, k < chunks - 3))
        def _():
            relay((k + 1) * halves)

        @pl.when(jnp.logical_and(relays, k == chunks - 3))
        def _():
            for n in range(whole, pieces):
                relay(n)

        load_weight(k).wait()
        chunk = gated[...].T
        for half in range(2):
            total[half] += jnp.dot(
                chunk,
                weight[rows_of(chunk_at(k)), half * cols : (half + 1) * cols],
                preferred_element_type=jnp.float32,
            )

    part_out[...] = total[other].astype(jnp.bfloat16)
    part_copy.start()
    load_weight(chunks - 1).wait()
    for i, (offset, size) in enumerate(tail):
        pl.when(jnp.logical_and(has_low, even))(lambda: wait_both(whole + i))
        wait_first(whole + i)
        for row in range(offset, offset + size, per_group):
            place = row - (channels - CHUNK)
            gated_tail[0, place : place + per_group, :] = gate(
                row, toeplitz[tail_ready + place // per_group], skip_wide[place : place + per_group, :]
            )
        place = offset - (channels - CHUNK)
        gated_copy(slice(place, place + size), min(i, 1)).start()

    total[core] += jnp.dot(
        gated_tail[0].T, weight[last_rows, half_cols(core)], preferred_element_type=jnp.float32
    )
    weight_copy.wait_recv()
    first_tail = slice(0, tail[0][1])
    rest_tail = slice(tail[0][1], CHUNK)
    gated_copy(first_tail, 0).wait_recv()
    total[core] += jnp.dot(
        gated_tail[1, first_tail].T, weight_in[first_tail], preferred_element_type=jnp.float32
    )

    everything = slice(0, channels)

    @pl.when(has_high)
    def _():
        far_copy(everything, 0).wait_send()

    @pl.when(even)
    def _():
        near_copy(everything, 0).wait_send()

    @pl.when(relays)
    def _():
        relay_copy(slice(0, channels - CHUNK), 0).wait_send()

    @pl.when(has_high)
    def _():
        lift_copy().wait_send()

    weight_copy.wait_send()
    part_copy.wait_send()
    gated_copy(slice(0, CHUNK), 0).wait_send()
    part_copy.wait_recv()
    gated_copy(rest_tail, 1).wait_recv()
    out_ref[...] = (
        total[core]
        + part_in[...].astype(jnp.float32)
        + jnp.dot(gated_tail[1, rest_tail].T, weight_in[rest_tail], preferred_element_type=jnp.float32)
    ).astype(jnp.bfloat16)


def piece_tail(channels):
    start = channels - CHUNK
    sizes = [PIECE] + [LAST] * ((CHUNK - PIECE) // LAST)
    return [(start + sum(sizes[:i]), size) for i, size in enumerate(sizes)]


def halo_body(
    query_feat,
    key_feat,
    value_feat,
    filter_seed,
    filter_in,
    filter_bias,
    filter_out,
    decay_rate,
    reach_blocks,
    skip_gain,
    out_weight,
):
    channels, block = query_feat.shape
    seq_count = lax.axis_size("seq")
    filters = decay_rate.shape[0]
    cols = out_weight.shape[1] // 2
    pieces = (channels - CHUNK) // PIECE + len(piece_tail(channels))
    small = (
        filter_seed.reshape(1, -1),
        filter_in,
        filter_bias.reshape(1, -1),
        filter_out,
        decay_rate.reshape(1, -1),
        reach_blocks.reshape(1, -1),
        skip_gain.reshape(-1, 128),
    )
    lags = block * 2
    return pl.pallas_call(
        functools.partial(halo_kernel, seq_count),
        out_shape=pltpu.VMEM((block, cols), jnp.bfloat16),
        in_specs=[pl.BlockSpec(memory_space=pltpu.HBM)] * 11,
        out_specs=pl.BlockSpec(memory_space=pltpu.VMEM),
        scratch_shapes=[
            *[pltpu.VMEM(array.shape, array.dtype) for array in small],
            pltpu.VMEM((channels, block), jnp.bfloat16),
            pltpu.VMEM((2, channels, block), jnp.bfloat16),
            pltpu.VMEM(out_weight.shape, jnp.bfloat16),
            pltpu.VMEM((channels, block), jnp.bfloat16),
            pltpu.VMEM((2, channels, block), jnp.bfloat16),
            pltpu.VMEM((CHUNK, block), jnp.bfloat16),
            pltpu.VMEM((filters, lags), jnp.float32),
            pltpu.VMEM(
                ((channels - READY * CHUNK) * filters // channels, 3 * block, block), jnp.bfloat16
            ),
            pltpu.VMEM((CHUNK, block), jnp.float32),
            pltpu.VMEM((CHUNK, block), jnp.bfloat16),
            pltpu.VMEM((2, CHUNK, block), jnp.bfloat16),
            pltpu.VMEM((CHUNK, cols), jnp.bfloat16),
            pltpu.VMEM((2, block, cols), jnp.float32),
            pltpu.VMEM((block, cols), jnp.bfloat16),
            pltpu.VMEM((block, cols), jnp.bfloat16),
            pltpu.SemaphoreType.DMA((len(small),)),
            pltpu.SemaphoreType.DMA,
            pltpu.SemaphoreType.DMA,
            pltpu.SemaphoreType.DMA((2,)),
            pltpu.SemaphoreType.DMA((3,)),
            pltpu.SemaphoreType.DMA((pieces,)),
            pltpu.SemaphoreType.DMA,
            pltpu.SemaphoreType.DMA((3,)),
            pltpu.SemaphoreType.DMA((4,)),
        ],
        compiler_params=pltpu.CompilerParams(
            collective_id=0, has_side_effects=True, vmem_limit_bytes=32 * 2**20
        ),
        name="halo_conv_project",
    )(
        *(
            pltpu.with_memory_space_constraint(array, pltpu.HBM)
            for array in (query_feat, key_feat, value_feat, *small, out_weight)
        )
    )


def filter_rows(
    lag_index,
    filter_seed,
    filter_in,
    filter_bias,
    filter_out,
    decay_rate,
    reach_blocks,
    block_len,
    seq_len,
    reach_max,
):
    safe_lag = jnp.maximum(lag_index, 0)
    phases = safe_lag[:, None] * filter_seed[None, :] % seq_len
    angles = phases.astype(jnp.float32) * (2.0 * math.pi / seq_len)
    features = jnp.concatenate([jnp.cos(angles), jnp.sin(angles)], axis=1)
    hidden = jnp.sin(
        jnp.dot(
            features, filter_in, precision=lax.Precision.HIGHEST, preferred_element_type=jnp.float32
        )
        + filter_bias
    )
    shaped = jnp.dot(
        hidden, filter_out, precision=lax.Precision.HIGHEST, preferred_element_type=jnp.float32
    )
    envelope = jnp.exp(-decay_rate[None, :] * safe_lag.astype(jnp.float32)[:, None]) * (
        1.0 / math.sqrt(reach_max * block_len)
    )
    inside = (lag_index[:, None] >= 0) & (lag_index[:, None] < reach_blocks[None, :] * block_len)
    return jnp.where(inside, shaped * envelope, 0.0).astype(jnp.bfloat16)


def hankel_rows(tap_rows, sub_len, span_len):
    return jnp.stack(
        [
            tap_rows[:, sub_len - 1 - offset : sub_len - 1 - offset + span_len]
            for offset in range(sub_len)
        ],
        axis=1,
    )


def body(
    query_feat,
    key_feat,
    value_feat,
    filter_seed,
    filter_in,
    filter_bias,
    filter_out,
    decay_rate,
    reach_blocks,
    skip_gain,
    out_weight,
):
    channels, block = query_feat.shape
    seq_count = lax.axis_size("seq")
    reach_max = seq_count // 4
    seq_len = block * seq_count
    sub_len = min(128, block)
    span_len = reach_max * block + sub_len
    rev_len = span_len + sub_len - 1
    filter_count = decay_rate.shape[0]
    per_group = channels // filter_count
    product = (key_feat.astype(jnp.float32) * value_feat.astype(jnp.float32)).astype(jnp.bfloat16)
    lag_index = reach_max * block + sub_len - 1 - lax.iota(jnp.int32, rev_len)
    taps = filter_rows(
        lag_index,
        filter_seed,
        filter_in,
        filter_bias,
        filter_out,
        decay_rate,
        reach_blocks,
        block,
        seq_len,
        reach_max,
    ).T
    seq_index = lax.axis_index("seq")
    spread, query_all = (
        lax.all_to_all(product, "seq", split_axis=0, concat_axis=1, tiled=True),
        lax.all_to_all(query_feat, "seq", split_axis=0, concat_axis=1, tiled=True),
    )
    chan_dev = spread.shape[0]
    full_len = spread.shape[1]
    padded = jnp.concatenate(
        [jnp.zeros((chan_dev, reach_max * block), jnp.bfloat16), spread], axis=1
    )
    pieces = padded.reshape(chan_dev, -1, sub_len)
    count_tiles = full_len // sub_len
    span_blocks = span_len // sub_len
    windows = jnp.concatenate([pieces[:, k : k + count_tiles] for k in range(span_blocks)], axis=2)
    first_chan = seq_index * chan_dev
    group_ids = (first_chan + lax.iota(jnp.int32, chan_dev)) // per_group
    chan_taps = jnp.take(taps, group_ids, axis=0)
    chan_block = math.gcd(8, chan_dev)
    windows = windows.reshape(chan_dev // chan_block, chan_block, count_tiles, span_len)
    chan_taps = chan_taps.reshape(chan_dev // chan_block, chan_block, rev_len)

    def convolve_chan(inputs_pair):
        window_part, tap_part = inputs_pair
        hankel = hankel_rows(tap_part, sub_len, span_len)
        return jnp.einsum("ctw,caw->cta", window_part, hankel, preferred_element_type=jnp.float32)

    convolved = lax.map(convolve_chan, (windows, chan_taps))
    convolved = convolved.reshape(chan_dev, full_len)
    skip_part = lax.dynamic_slice_in_dim(skip_gain, first_chan, chan_dev)
    mixed_part = convolved + skip_part[:, None] * spread.astype(jnp.float32)
    gated_part = (query_all.astype(jnp.float32) * mixed_part).astype(jnp.bfloat16)
    gated = lax.all_to_all(gated_part, "seq", split_axis=1, concat_axis=0, tiled=True)
    reduced = lax.psum_scatter(
        lax.dot_general(
            out_weight, gated, (((0,), (0,)), ((), ())), preferred_element_type=jnp.float32
        ),
        "chan",
        scatter_dimension=0,
        tiled=True,
    )
    return reduced.T.astype(jnp.bfloat16)


def solution(mesh):
    halo = mesh.shape["seq"] // 4 == 2 and mesh.shape["chan"] == 2
    return jax.shard_map(
        halo_body if halo else body,
        mesh=mesh,
        in_specs=(
            P("chan", ("groups", "seq")),
            P("chan", ("groups", "seq")),
            P("chan", ("groups", "seq")),
            P(),
            P(),
            P(),
            P(None, "chan"),
            P("chan"),
            P("chan"),
            P("chan"),
            P("chan", None),
        ),
        out_specs=P(("groups", "seq"), "chan"),
        check_vma=False,
    )
```

```python
import functools
import math

import jax
import jax.numpy as jnp
from jax import lax
from jax.experimental import pallas as pl
from jax.experimental.pallas import tpu as pltpu
from jax.sharding import PartitionSpec as P

MESH = pl.DeviceIdType.MESH
CHUNK = 256
PIECE = 128
LAST = 128
EARLY = 6
READY = 4
CARRY_AT = 5


def as_column(row, size):
    rows = lax.broadcasted_iota(jnp.int32, (size, size), 0)
    cols = lax.broadcasted_iota(jnp.int32, (size, size), 1)
    spread = jnp.broadcast_to(row, (size, size))
    return jnp.sum(jnp.where(rows == cols, spread, 0.0), axis=1, keepdims=True)


def halo_kernel(
    seq_count,
    query_hbm,
    key_hbm,
    value_hbm,
    seed_hbm,
    in_hbm,
    bias_hbm,
    fout_hbm,
    decay_hbm,
    reach_hbm,
    skip_hbm,
    weight_hbm,
    out_ref,
    seed_ref,
    in_ref,
    bias_ref,
    fout_ref,
    decay_ref,
    reach_ref,
    skip_ref,
    query,
    factors,
    weight,
    product,
    back,
    lifted,
    taps,
    toeplitz,
    skip_wide,
    gated,
    gated_tail,
    weight_in,
    total,
    part_out,
    part_in,
    small_sem,
    factor_sem,
    query_sem,
    weight_sem,
    send_sem,
    arrive_sem,
    lift_sem,
    core_send,
    core_recv,
):
    channels, block = product.shape
    filters = taps.shape[0]
    per_group = channels // filters
    lags = taps.shape[1]
    chunks = channels // CHUNK
    halves = CHUNK // PIECE
    groups_piece = PIECE // per_group
    cols = out_ref.shape[1]
    seq_len = seq_count * block
    whole = (channels - CHUNK) // PIECE
    tail = piece_tail(channels)
    pieces = whole + len(tail)
    carried = list(range(whole - halves, whole))
    carried_rows = slice(channels - 2 * CHUNK, channels - CHUNK)
    order = [n for n in range(pieces) if n not in carried] + carried

    me = lax.axis_index("seq")
    core = lax.axis_index("chan")
    pair = me // 2
    odd = me % 2
    mate = me + 1 - 2 * odd
    other = 1 - core
    has_low = pair > 0
    has_high = pair < seq_count // 2 - 1
    even = odd == 0
    relays = jnp.logical_and(has_low, odd == 1)
    carries = jnp.logical_and(has_high, even)

    barrier = pltpu.get_barrier_semaphore()

    def greet(device):
        pl.semaphore_signal(barrier, inc=1, device_id=device, device_id_type=MESH)

    greet({"chan": other})
    greet({"seq": mate})
    pl.when(has_low)(lambda: greet({"seq": me - 2}))
    receivers = 2 + has_high.astype(jnp.int32)

    def rows_of(k):
        return pl.ds(pl.multiple_of(k * CHUNK, CHUNK), CHUNK)

    def piece_of(n):
        if isinstance(n, int) and n >= whole:
            return pl.ds(*tail[n - whole])
        return pl.ds(pl.multiple_of(n * PIECE, PIECE), PIECE)

    def chunk_at(k):
        lifted_chunk = chunks - 2
        moved = jnp.where(k == CARRY_AT, lifted_chunk, jnp.where(k > CARRY_AT, k - 1, k))
        return jnp.where(jnp.logical_and(even, k <= lifted_chunk), moved, k)

    def load_weight(k):
        rows = rows_of(chunk_at(k))
        return pltpu.make_async_copy(weight_hbm.at[rows], weight.at[rows], weight_sem.at[k % 2])

    load_key = pltpu.make_async_copy(key_hbm, factors.at[0], factor_sem)
    load_value = pltpu.make_async_copy(value_hbm, factors.at[1], factor_sem)
    load_query = pltpu.make_async_copy(query_hbm, query, query_sem)

    def far_copy(rows, n):
        return pltpu.make_async_remote_copy(
            src_ref=product.at[rows],
            dst_ref=back.at[0, rows],
            send_sem=send_sem.at[0],
            recv_sem=arrive_sem.at[n],
            device_id={"seq": me + 2},
            device_id_type=MESH,
        )

    def near_copy(rows, n):
        return pltpu.make_async_remote_copy(
            src_ref=product.at[rows],
            dst_ref=back.at[1, rows],
            send_sem=send_sem.at[1],
            recv_sem=arrive_sem.at[n],
            device_id={"seq": mate},
            device_id_type=MESH,
        )

    def relay_copy(rows, n):
        return pltpu.make_async_remote_copy(
            src_ref=back.at[0, rows],
            dst_ref=back.at[1, rows],
            send_sem=send_sem.at[1],
            recv_sem=arrive_sem.at[n],
            device_id={"seq": mate},
            device_id_type=MESH,
        )

    def lift_copy():
        return pltpu.make_async_remote_copy(
            src_ref=product.at[carried_rows],
            dst_ref=lifted,
            send_sem=send_sem.at[2],
            recv_sem=lift_sem,
            device_id={"seq": mate},
            device_id_type=MESH,
        )

    def carry_copy(i):
        return pltpu.make_async_remote_copy(
            src_ref=lifted.at[pl.ds(i * PIECE, PIECE)],
            dst_ref=back.at[1, piece_of(carried[i])],
            send_sem=send_sem.at[2],
            recv_sem=arrive_sem.at[carried[i]],
            device_id={"seq": me + 2},
            device_id_type=MESH,
        )

    last_rows = slice(channels - CHUNK, channels)

    def half_cols(half):
        return pl.ds(pl.multiple_of(half * cols, cols), cols)

    weight_copy = pltpu.make_async_remote_copy(
        src_ref=weight_hbm.at[last_rows, half_cols(other)],
        dst_ref=weight_in,
        send_sem=core_send.at[0],
        recv_sem=core_recv.at[0],
        device_id={"chan": other},
        device_id_type=MESH,
    )
    part_copy = pltpu.make_async_remote_copy(
        src_ref=part_out,
        dst_ref=part_in,
        send_sem=core_send.at[1],
        recv_sem=core_recv.at[1],
        device_id={"chan": other},
        device_id_type=MESH,
    )

    def gated_copy(rows, i):
        return pltpu.make_async_remote_copy(
            src_ref=gated_tail.at[0, rows],
            dst_ref=gated_tail.at[1, rows],
            send_sem=core_send.at[2],
            recv_sem=core_recv.at[2 + i],
            device_id={"chan": other},
            device_id_type=MESH,
        )

    load_key.start()
    load_value.start()
    small = [
        pltpu.make_async_copy(source, target, small_sem.at[i])
        for i, (source, target) in enumerate(
            (
                (seed_hbm, seed_ref),
                (in_hbm, in_ref),
                (bias_hbm, bias_ref),
                (fout_hbm, fout_ref),
                (decay_hbm, decay_ref),
                (reach_hbm, reach_ref),
                (skip_hbm, skip_ref),
            )
        )
    ]
    for copy in small:
        copy.start()

    pltpu.make_async_copy(factors, factors, factor_sem).wait()

    def multiply(rows):
        part = factors[0, rows].astype(jnp.float32) * factors[1, rows].astype(jnp.float32)
        product[rows] = part.astype(jnp.bfloat16)

    def start_far(first, last):
        for n in order[first:last]:
            far_copy(piece_of(n), n).start()

    def start_near(first, last):
        for n in order[first:last]:
            near_copy(piece_of(n), n).start()

    half_rows = EARLY * PIECE
    multiply(slice(0, half_rows))
    multiply(carried_rows)
    pl.semaphore_wait(barrier, receivers)

    @pl.when(jnp.logical_and(odd == 1, has_high))
    def _():
        far_copy(piece_of(0), 0).start()
        lift_copy().start()
        start_far(1, EARLY)

    @pl.when(carries)
    def _():
        for n in range(EARLY):
            far_copy(piece_of(n), n).start()
            near_copy(piece_of(n), n).start()

    @pl.when(jnp.logical_and(even, jnp.logical_not(has_high)))
    def _():
        start_near(0, EARLY)

    multiply(slice(half_rows, channels - 2 * CHUNK))
    multiply(slice(channels - CHUNK, channels))

    @pl.when(jnp.logical_and(odd == 1, has_high))
    def _():
        start_far(EARLY, pieces)

    @pl.when(even)
    def _():
        start_near(EARLY, pieces)

    load_query.start()
    load_weight(0).start()
    weight_copy.start()
    for copy in small:
        copy.wait()

    @pl.when(jnp.logical_not(has_low))
    def _():
        back[0] = jnp.zeros_like(back[0])

    @pl.when(me == 0)
    def _():
        back[1] = jnp.zeros_like(back[1])

    freqs = in_ref.shape[0] // 2
    hidden_count = in_ref.shape[1]
    lag = lax.broadcasted_iota(jnp.int32, (freqs, lags), 1)
    seeds = as_column(seed_ref[...].astype(jnp.float32), freqs).astype(jnp.int32)
    angles = ((seeds * lag) & (seq_len - 1)).astype(jnp.float32) * (2.0 * math.pi / seq_len)
    features = jnp.concatenate([jnp.cos(angles), jnp.sin(angles)], axis=0)
    first_dims = (((0,), (0,)), ((), ()))
    hidden = jnp.sin(
        lax.dot_general(
            in_ref[...],
            features,
            first_dims,
            precision=lax.Precision.HIGHEST,
            preferred_element_type=jnp.float32,
        )
        + as_column(bias_ref[...], hidden_count)
    )
    shaped = lax.dot_general(
        fout_ref[...],
        hidden,
        first_dims,
        precision=lax.Precision.HIGHEST,
        preferred_element_type=jnp.float32,
    )
    lag = lax.broadcasted_iota(jnp.int32, (filters, lags), 1).astype(jnp.float32)
    envelope = jnp.exp(-as_column(decay_ref[...], filters) * lag) * (1.0 / math.sqrt(lags))
    inside = lag < as_column(reach_ref[...].astype(jnp.float32), filters) * block
    taps[...] = (
        jnp.where(inside, shaped * envelope, 0.0).astype(jnp.bfloat16).astype(jnp.float32)
    )

    total[...] = jnp.zeros_like(total)
    load_query.wait()
    source_tok = lax.broadcasted_iota(jnp.int32, (block, block), 0)
    target_tok = lax.broadcasted_iota(jnp.int32, (block, block), 1)
    upper = target_tok >= source_tok

    def spread(row):
        return pltpu.roll(
            jnp.broadcast_to(row, (block, block)), 0, 1, stride=1, stride_axis=0
        ).astype(jnp.bfloat16)

    def band(group):
        tap_row = taps[pl.ds(group, 1), :]
        low = spread(tap_row[:, :block])
        high = spread(tap_row[:, block:])
        zero = jnp.zeros_like(low)
        return (
            jnp.where(upper, zero, high),
            jnp.where(upper, high, low),
            jnp.where(upper, low, zero),
        )

    def skip_rows(n):
        return jnp.broadcast_to(skip_ref[pl.ds(n, 1), :], (PIECE, PIECE)).T

    for n in range(halves):
        skip_wide[n * PIECE : (n + 1) * PIECE, :] = skip_rows(whole + n)
    first_ready = READY * CHUNK // per_group
    tail_ready = (channels - CHUNK) // per_group - first_ready

    def make_ready(slot):
        for i, part in enumerate(band(first_ready + slot)):
            toeplitz[slot, i * block : (i + 1) * block] = part

    for j in range(CHUNK // per_group):
        make_ready(tail_ready + j)

    @pl.when(carries)
    def _():
        lift_copy().wait_recv()
        for i in range(halves):
            carry_copy(i).start()
        for n in range(EARLY, pieces):
            far_copy(piece_of(n), n).start()

    @pl.when(even)
    def _():
        @pl.loop(0, tail_ready // groups_piece)
        def _(i):
            for j in range(groups_piece):
                make_ready(i * groups_piece + j)

    def wait_both(n):
        both = back.at[:, piece_of(n)]
        pltpu.make_async_copy(both, both, arrive_sem.at[n]).wait()

    def wait_first(n):
        @pl.when(me == 1)
        def _():
            near_copy(piece_of(n), n).wait_recv()

    def relay(n):
        wait_both(n)
        relay_copy(piece_of(n), n).start()

    def arrive(n, first):
        ahead = jnp.logical_and(relays, n < carried[0])
        pl.when(jnp.logical_and(has_low, jnp.logical_not(ahead)))(lambda: wait_both(n))
        wait_first(n)
        if not first:
            pl.when(ahead)(lambda: relay(n))

    def gate(row, matrix, skip):
        rows = pl.ds(pl.multiple_of(row, per_group), per_group)
        own = product[rows, :]
        window = jnp.concatenate([back[0, rows, :], back[1, rows, :], own], axis=1)
        mixed = jnp.dot(window, matrix, preferred_element_type=jnp.float32)
        mixed = mixed + skip * own.astype(jnp.float32)
        return (query[rows, :].astype(jnp.float32) * mixed).astype(jnp.bfloat16)

    pl.when(relays)(lambda: relay(0))

    @pl.loop(0, chunks - 1)
    def _(k):
        load_weight(k + 1).start()

        for half in range(halves):
            n = chunk_at(k) * halves + half
            arrive(n, half == 0)
            ready = jnp.logical_and(even, k >= READY)

            def convolve(matrix_of):
                skip = skip_rows(n)
                for j in range(groups_piece):
                    start = j * per_group
                    place = half * PIECE + start
                    gated[place : place + per_group, :] = gate(
                        n * PIECE + start,
                        matrix_of(n * groups_piece + j),
                        skip[start : start + per_group],
                    )

            @pl.when(ready)
            def _():
                convolve(lambda group: toeplitz[group - first_ready])

            @pl.when(jnp.logical_not(ready))
            def _():
                convolve(lambda group: jnp.concatenate(band(group), axis=0))

        @pl.when(jnp.logical_and(relays, k < chunks - 3))
        def _():
            relay((k + 1) * halves)

        @pl.when(jnp.logical_and(relays, k == chunks - 3))
        def _():
            for n in range(whole, pieces):
                relay(n)

        load_weight(k).wait()
        chunk = gated[...].T
        for half in range(2):
            total[half] += jnp.dot(
                chunk,
                weight[rows_of(chunk_at(k)), half * cols : (half + 1) * cols],
                preferred_element_type=jnp.float32,
            )

    part_out[...] = total[other].astype(jnp.bfloat16)
    part_copy.start()
    load_weight(chunks - 1).wait()
    for i, (offset, size) in enumerate(tail):
        pl.when(jnp.logical_and(has_low, even))(lambda: wait_both(whole + i))
        wait_first(whole + i)
        for row in range(offset, offset + size, per_group):
            place = row - (channels - CHUNK)
            gated_tail[0, place : place + per_group, :] = gate(
                row, toeplitz[tail_ready + place // per_group], skip_wide[place : place + per_group, :]
            )
        place = offset - (channels - CHUNK)
        gated_copy(slice(place, place + size), min(i, 1)).start()

    total[core] += jnp.dot(
        gated_tail[0].T, weight[last_rows, half_cols(core)], preferred_element_type=jnp.float32
    )
    weight_copy.wait_recv()
    first_tail = slice(0, tail[0][1])
    rest_tail = slice(tail[0][1], CHUNK)
    gated_copy(first_tail, 0).wait_recv()
    total[core] += jnp.dot(
        gated_tail[1, first_tail].T, weight_in[first_tail], preferred_element_type=jnp.float32
    )

    everything = slice(0, channels)

    @pl.when(has_high)
    def _():
        far_copy(everything, 0).wait_send()

    @pl.when(even)
    def _():
        near_copy(everything, 0).wait_send()

    @pl.when(relays)
    def _():
        relay_copy(slice(0, channels - CHUNK), 0).wait_send()

    @pl.when(has_high)
    def _():
        lift_copy().wait_send()

    weight_copy.wait_send()
    part_copy.wait_send()
    gated_copy(slice(0, CHUNK), 0).wait_send()
    part_copy.wait_recv()
    gated_copy(rest_tail, 1).wait_recv()
    out_ref[...] = (
        total[core]
        + part_in[...].astype(jnp.float32)
        + jnp.dot(gated_tail[1, rest_tail].T, weight_in[rest_tail], preferred_element_type=jnp.float32)
    ).astype(jnp.bfloat16)


def piece_tail(channels):
    start = channels - CHUNK
    sizes = [PIECE] + [LAST] * ((CHUNK - PIECE) // LAST)
    return [(start + sum(sizes[:i]), size) for i, size in enumerate(sizes)]


def halo_body(
    query_feat,
    key_feat,
    value_feat,
    filter_seed,
    filter_in,
    filter_bias,
    filter_out,
    decay_rate,
    reach_blocks,
    skip_gain,
    out_weight,
):
    channels, block = query_feat.shape
    seq_count = lax.axis_size("seq")
    filters = decay_rate.shape[0]
    cols = out_weight.shape[1] // 2
    pieces = (channels - CHUNK) // PIECE + len(piece_tail(channels))
    small = (
        filter_seed.reshape(1, -1),
        filter_in,
        filter_bias.reshape(1, -1),
        filter_out,
        decay_rate.reshape(1, -1),
        reach_blocks.reshape(1, -1),
        skip_gain.reshape(-1, 128),
    )
    lags = block * 2
    return pl.pallas_call(
        functools.partial(halo_kernel, seq_count),
        out_shape=pltpu.VMEM((block, cols), jnp.bfloat16),
        in_specs=[pl.BlockSpec(memory_space=pltpu.HBM)] * 11,
        out_specs=pl.BlockSpec(memory_space=pltpu.VMEM),
        scratch_shapes=[
            *[pltpu.VMEM(array.shape, array.dtype) for array in small],
            pltpu.VMEM((channels, block), jnp.bfloat16),
            pltpu.VMEM((2, channels, block), jnp.bfloat16),
            pltpu.VMEM(out_weight.shape, jnp.bfloat16),
            pltpu.VMEM((channels, block), jnp.bfloat16),
            pltpu.VMEM((2, channels, block), jnp.bfloat16),
            pltpu.VMEM((CHUNK, block), jnp.bfloat16),
            pltpu.VMEM((filters, lags), jnp.float32),
            pltpu.VMEM(
                ((channels - READY * CHUNK) * filters // channels, 3 * block, block), jnp.bfloat16
            ),
            pltpu.VMEM((CHUNK, block), jnp.float32),
            pltpu.VMEM((CHUNK, block), jnp.bfloat16),
            pltpu.VMEM((2, CHUNK, block), jnp.bfloat16),
            pltpu.VMEM((CHUNK, cols), jnp.bfloat16),
            pltpu.VMEM((2, block, cols), jnp.float32),
            pltpu.VMEM((block, cols), jnp.bfloat16),
            pltpu.VMEM((block, cols), jnp.bfloat16),
            pltpu.SemaphoreType.DMA((len(small),)),
            pltpu.SemaphoreType.DMA,
            pltpu.SemaphoreType.DMA,
            pltpu.SemaphoreType.DMA((2,)),
            pltpu.SemaphoreType.DMA((3,)),
            pltpu.SemaphoreType.DMA((pieces,)),
            pltpu.SemaphoreType.DMA,
            pltpu.SemaphoreType.DMA((3,)),
            pltpu.SemaphoreType.DMA((4,)),
        ],
        compiler_params=pltpu.CompilerParams(
            collective_id=0, has_side_effects=True, vmem_limit_bytes=32 * 2**20
        ),
        name="halo_conv_project",
    )(
        *(
            pltpu.with_memory_space_constraint(array, pltpu.HBM)
            for array in (query_feat, key_feat, value_feat, *small, out_weight)
        )
    )


def filter_rows(
    lag_index,
    filter_seed,
    filter_in,
    filter_bias,
    filter_out,
    decay_rate,
    reach_blocks,
    block_len,
    seq_len,
    reach_max,
):
    safe_lag = jnp.maximum(lag_index, 0)
    phases = safe_lag[:, None] * filter_seed[None, :] % seq_len
    angles = phases.astype(jnp.float32) * (2.0 * math.pi / seq_len)
    features = jnp.concatenate([jnp.cos(angles), jnp.sin(angles)], axis=1)
    hidden = jnp.sin(
        jnp.dot(
            features, filter_in, precision=lax.Precision.HIGHEST, preferred_element_type=jnp.float32
        )
        + filter_bias
    )
    shaped = jnp.dot(
        hidden, filter_out, precision=lax.Precision.HIGHEST, preferred_element_type=jnp.float32
    )
    envelope = jnp.exp(-decay_rate[None, :] * safe_lag.astype(jnp.float32)[:, None]) * (
        1.0 / math.sqrt(reach_max * block_len)
    )
    inside = (lag_index[:, None] >= 0) & (lag_index[:, None] < reach_blocks[None, :] * block_len)
    return jnp.where(inside, shaped * envelope, 0.0).astype(jnp.bfloat16)


def hankel_rows(tap_rows, sub_len, span_len):
    return jnp.stack(
        [
            tap_rows[:, sub_len - 1 - offset : sub_len - 1 - offset + span_len]
            for offset in range(sub_len)
        ],
        axis=1,
    )


def body(
    query_feat,
    key_feat,
    value_feat,
    filter_seed,
    filter_in,
    filter_bias,
    filter_out,
    decay_rate,
    reach_blocks,
    skip_gain,
    out_weight,
):
    channels, block = query_feat.shape
    seq_count = lax.axis_size("seq")
    reach_max = seq_count // 4
    seq_len = block * seq_count
    sub_len = min(128, block)
    span_len = reach_max * block + sub_len
    rev_len = span_len + sub_len - 1
    filter_count = decay_rate.shape[0]
    per_group = channels // filter_count
    product = (key_feat.astype(jnp.float32) * value_feat.astype(jnp.float32)).astype(jnp.bfloat16)
    lag_index = reach_max * block + sub_len - 1 - lax.iota(jnp.int32, rev_len)
    taps = filter_rows(
        lag_index,
        filter_seed,
        filter_in,
        filter_bias,
        filter_out,
        decay_rate,
        reach_blocks,
        block,
        seq_len,
        reach_max,
    ).T
    seq_index = lax.axis_index("seq")
    spread, query_all = (
        lax.all_to_all(product, "seq", split_axis=0, concat_axis=1, tiled=True),
        lax.all_to_all(query_feat, "seq", split_axis=0, concat_axis=1, tiled=True),
    )
    chan_dev = spread.shape[0]
    full_len = spread.shape[1]
    padded = jnp.concatenate(
        [jnp.zeros((chan_dev, reach_max * block), jnp.bfloat16), spread], axis=1
    )
    pieces = padded.reshape(chan_dev, -1, sub_len)
    count_tiles = full_len // sub_len
    span_blocks = span_len // sub_len
    windows = jnp.concatenate([pieces[:, k : k + count_tiles] for k in range(span_blocks)], axis=2)
    first_chan = seq_index * chan_dev
    group_ids = (first_chan + lax.iota(jnp.int32, chan_dev)) // per_group
    chan_taps = jnp.take(taps, group_ids, axis=0)
    chan_block = math.gcd(8, chan_dev)
    windows = windows.reshape(chan_dev // chan_block, chan_block, count_tiles, span_len)
    chan_taps = chan_taps.reshape(chan_dev // chan_block, chan_block, rev_len)

    def convolve_chan(inputs_pair):
        window_part, tap_part = inputs_pair
        hankel = hankel_rows(tap_part, sub_len, span_len)
        return jnp.einsum("ctw,caw->cta", window_part, hankel, preferred_element_type=jnp.float32)

    convolved = lax.map(convolve_chan, (windows, chan_taps))
    convolved = convolved.reshape(chan_dev, full_len)
    skip_part = lax.dynamic_slice_in_dim(skip_gain, first_chan, chan_dev)
    mixed_part = convolved + skip_part[:, None] * spread.astype(jnp.float32)
    gated_part = (query_all.astype(jnp.float32) * mixed_part).astype(jnp.bfloat16)
    gated = lax.all_to_all(gated_part, "seq", split_axis=1, concat_axis=0, tiled=True)
    reduced = lax.psum_scatter(
        lax.dot_general(
            out_weight, gated, (((0,), (0,)), ((), ())), preferred_element_type=jnp.float32
        ),
        "chan",
        scatter_dimension=0,
        tiled=True,
    )
    return reduced.T.astype(jnp.bfloat16)


def solution(mesh):
    halo = mesh.shape["seq"] // 4 == 2 and mesh.shape["chan"] == 2
    return jax.shard_map(
        halo_body if halo else body,
        mesh=mesh,
        in_specs=(
            P("chan", ("groups", "seq")),
            P("chan", ("groups", "seq")),
            P("chan", ("groups", "seq")),
            P(),
            P(),
            P(),
            P(None, "chan"),
            P("chan"),
            P("chan"),
            P("chan"),
            P("chan", None),
        ),
        out_specs=P(("groups", "seq"), "chan"),
        check_vma=False,
    )
```
